32 devices in a mesh: narrow: 2 (over x), wide: 16 (over z, y, core).
Axes of the slice: x: 2, y: 2, z: 4, core: 2. Of those that a mesh axis runs over, the one named last changes fastest.
Arguments:
- state: float32 [1280, 1280], P('wide', 'narrow'), may hold values from 0 to 10, as said below
- in_pattern: int32 [5, 5], replicated, may hold values from 0 to 1, as said below
- out_pattern: int32 [5, 5], replicated, may hold values from 0 to 1, as said below
Outputs:
- clustered: float32 [1280, 1280], P('wide', 'narrow')
The draws below stay inside these ranges and needn't reach their ends.
Inputs may be any that keep to these rules, and one draw needn't show every extreme that they name: `in_pattern`: entries are 0 or 1 and every diagonal block is 1. `out_pattern`: entries are 0 or 1 and every diagonal block is 1. `state`: nonnegative; the diagonal lies between 0.5 and 1.
All inputs are finite; a program needn't handle non-finite values.
Results may differ from the reference program's by a relative error of at most 0.00011.
Values sent between devices are 32-bit elements; how exact they have to be, the bound alone decides.
A program may use at most 64 MiB of HBM per device.

```python
import jax
import jax.numpy as jnp
from jax import lax

BLK = 256
NODES = 1280
NBLK = 5


def draw_state(key, part):
    key = jax.random.fold_in(key, 1)
    key_live, key_vals, key_diag = jax.random.split(key, 3)
    live = (jax.random.randint(key_live, (NODES, NODES), 0, 2) == 0).astype(jnp.float32)
    vals = jnp.exp(jax.random.uniform(key_vals, (NODES, NODES), jnp.float32, -6.9, 0.0))
    diag = jax.random.uniform(key_diag, (NODES, 1), jnp.float32, 0.5, 1.0)
    rows = jnp.arange(NODES)[:, None]
    cols = jnp.arange(NODES)[None, :]
    return jnp.where(rows == cols, diag, vals * live)


def draw_in_pattern(key, part):
    key = jax.random.fold_in(key, 2)
    picks = (jax.random.randint(key, (NBLK, NBLK), 0, 8) < 3).astype(jnp.int32)
    return jnp.maximum(picks, jnp.eye(NBLK, dtype=jnp.int32))


def draw_out_pattern(key, part):
    key = jax.random.fold_in(key, 3)
    picks = (jax.random.randint(key, (NBLK, NBLK), 0, 8) < 5).astype(jnp.int32)
    return jnp.maximum(picks, jnp.eye(NBLK, dtype=jnp.int32))


def setup_inputs(seed: int = 0) -> dict:
    streams_of = jax.random.split(jax.random.key(seed), 4)
    return {
        "state": draw_state(jax.random.fold_in(streams_of[3], 71), 0),
        "in_pattern": draw_in_pattern(jax.random.fold_in(streams_of[3], 71), 0),
        "out_pattern": draw_out_pattern(jax.random.fold_in(streams_of[3], 71), 0),
    }


def expand_pattern(pattern):
    grown = jnp.repeat(jnp.repeat(pattern.astype(jnp.float32), BLK, axis=0), BLK, axis=1)
    return grown


def reference(state, in_pattern, out_pattern):
    masked = state * expand_pattern(in_pattern)
    expanded = jnp.dot(masked, masked, preferred_element_type=jnp.float32, precision=lax.Precision.HIGHEST)
    inflated = expanded * expanded * expand_pattern(out_pattern)
    totals = jnp.sum(inflated, axis=1)
    return inflated * (NODES / totals)[:, None]
```

```python
import functools

import jax
import jax.numpy as jnp
from jax import lax
from jax.experimental import pallas as pl
from jax.experimental.pallas import tpu as pltpu
from jax.sharding import PartitionSpec as P

BLK = 256
LANES = 128
MESH = pl.DeviceIdType.MESH
UP, DOWN, ACROSS, SIBLING = range(4)


def split(value):
    high = value.astype(jnp.bfloat16)
    low = (value - high.astype(jnp.float32)).astype(jnp.bfloat16)
    return high, low


def kernel(
    narrow, wide, parts, in_ref, out_pat_ref, x_ref, o_ref,
    blocks, row_parts, sums, send_sem, recv_sem,
    row_send, row_recv, sum_send, sum_recv,
):
    rows, cols = x_ref.shape
    blks = in_ref.shape[0]
    units = cols // LANES
    line = wide // 4
    group = wide // narrow
    n = lax.axis_index("narrow")
    w = lax.axis_index("wide")
    z, y, c = w // 4, (w // 2) % 2, w % 2

    def index(zz, yy, cc):
        return (zz * 2 + yy) * 2 + cc

    def partner(kind):
        return {
            UP: (n, index(z + 1, y, c)),
            DOWN: (n, index(z - 1, y, c)),
            ACROSS: (n, index(z, 1 - y, c)),
            SIBLING: (n, index(z, y, 1 - c)),
        }[kind]

    has_up, has_down = z + 1 < line, z >= 1
    others = [lax.rem(n + d, narrow) for d in range(1, narrow)]

    barrier = pltpu.get_barrier_semaphore()

    def greet(device):
        pl.semaphore_signal(barrier, inc=1, device_id=device, device_id_type=MESH)

    greet(partner(ACROSS))
    greet(partner(SIBLING))
    for other in others:
        greet((other, w))

    @pl.when(has_up)
    def _():
        greet(partner(UP))

    @pl.when(has_down)
    def _():
        greet(partner(DOWN))

    first = (w * rows) // BLK
    second = jnp.minimum(first + 1, blks - 1)
    upper = lax.broadcasted_iota(jnp.int32, (rows, LANES), 0) < (first + 1) * BLK - w * rows

    def keep(pattern, u):
        col = (n * cols + u * LANES) // BLK
        return jnp.where(
            upper, pattern[first, col].astype(jnp.float32), pattern[second, col].astype(jnp.float32)
        )

    for u in range(units):
        at = slice(u * LANES, (u + 1) * LANES)
        masked = x_ref[:, at] * keep(in_ref, u)
        blocks[w, :, at] = masked
        row_parts[n, :, at] = masked

    met = 1 + 1 + len(others) + has_up.astype(jnp.int32) + has_down.astype(jnp.int32)
    pl.semaphore_wait(barrier, met)

    def copy(kind, slot, part):
        start, size, _ = parts[part]
        ref = blocks.at[slot, pl.ds(start, size), :]
        return pltpu.make_async_remote_copy(
            src_ref=ref,
            dst_ref=ref,
            send_sem=send_sem.at[kind, slot, part],
            recv_sem=recv_sem.at[slot, part],
            device_id=partner(kind),
            device_id_type=MESH,
        )

    def arrive(slot, part):
        copy(SIBLING, slot, part).wait_recv()

    def go(kind, slot, part, act):
        if kind == UP:
            pl.when(has_up)(lambda: act(copy(kind, slot, part)))
        elif kind == DOWN:
            pl.when(has_down)(lambda: act(copy(kind, slot, part)))
        else:
            act(copy(kind, slot, part))

    def row_copy(other):
        return pltpu.make_async_remote_copy(
            src_ref=blocks.at[w],
            dst_ref=row_parts.at[n],
            send_sem=row_send.at[other],
            recv_sem=row_recv.at[n],
            device_id=(other, w),
            device_id_type=MESH,
        )

    def row_arrival(other):
        return pltpu.make_async_remote_copy(
            src_ref=blocks.at[w],
            dst_ref=row_parts.at[other],
            send_sem=row_send.at[other],
            recv_sem=row_recv.at[other],
            device_id=(other, w),
            device_id_type=MESH,
        )

    def walk(visit):
        count = len(parts)
        for part in range(count):
            visit(None, w, part, (UP, DOWN, ACROSS, SIBLING), True)
        across = [p for p in range(count) if parts[p][2]]
        along = [p for p in range(count) if not parts[p][2]]
        for part in across:
            visit(None, index(z, 1 - y, c), part, (UP, DOWN, SIBLING), False)
        for part in along:
            visit(None, index(z, 1 - y, c), part, (SIBLING,), False)
        for step in range(1, line):
            for part in along:
                visit(z >= step, index(z - step, y, c), part, (UP, ACROSS, SIBLING), False)
                visit(z + step < line, index(z + step, y, c), part, (DOWN, ACROSS, SIBLING), False)
            for part in across:
                for yy in (y, 1 - y):
                    visit(z >= step, index(z - step, yy, c), part, (UP, SIBLING), False)
                    visit(z + step < line, index(z + step, yy, c), part, (DOWN, SIBLING), False)
            for part in along:
                visit(z >= step, index(z - step, 1 - y, c), part, (SIBLING,), False)
                visit(z + step < line, index(z + step, 1 - y, c), part, (SIBLING,), False)

    def under(condition, act):
        if condition is None:
            act()
        else:
            pl.when(condition)(act)

    def forward(condition, slot, part, kinds, mine):
        def act():
            if not mine:
                arrive(slot, part)
            for kind in kinds:
                go(kind, slot, part, lambda one: one.start())

        under(condition, act)
        if mine and part == len(parts) - 1:
            for other in others:
                row_copy(other).start()

    walk(forward)
    for zz in range(line):
        for yy in range(2):
            for part in range(len(parts)):
                arrive(index(zz, yy, 1 - c), part)
    for other in others:
        row_arrival(other).wait_recv()

    expanded = None
    for g in range(narrow):
        a_high, a_low = split(row_parts[g])
        both = jnp.concatenate([a_high, a_low], axis=0)
        b_high, b_low = split(blocks[pl.ds(g * group, group)].reshape(group * rows, cols))
        first_two = jnp.dot(both, b_high, preferred_element_type=jnp.float32)
        term = first_two[:rows] + first_two[rows:]
        term = term + jnp.dot(a_high, b_low, preferred_element_type=jnp.float32)
        expanded = term if expanded is None else expanded + term

    partial = None
    for u in range(units):
        at = slice(u * LANES, (u + 1) * LANES)
        inflated = expanded[:, at] * expanded[:, at] * keep(out_pat_ref, u)
        o_ref[:, at] = inflated
        partial = inflated if partial is None else partial + inflated
    sums[n] = partial

    def sum_copy(other, slot):
        return pltpu.make_async_remote_copy(
            src_ref=sums.at[n],
            dst_ref=sums.at[slot],
            send_sem=sum_send.at[other],
            recv_sem=sum_recv.at[slot],
            device_id=(other, w),
            device_id_type=MESH,
        )

    for other in others:
        sum_copy(other, n).start()

    def drain(condition, slot, part, kinds, mine):
        under(condition, lambda: [go(kind, slot, part, lambda one: one.wait_send()) for kind in kinds] and None)

    walk(drain)
    for other in others:
        row_copy(other).wait_send()
    for other in others:
        sum_copy(other, other).wait_recv()
    total = sums[0]
    for g in range(1, narrow):
        total = total + sums[g]
    scale = (cols * narrow) / jnp.sum(total, axis=1, keepdims=True)
    o_ref[...] = o_ref[...] * scale
    for other in others:
        sum_copy(other, n).wait_send()


def body(narrow, wide, state, in_pattern, out_pattern):
    rows, cols = state.shape
    part = rows // 80 * 64 if rows % 80 == 0 else rows // 2
    parts = ((0, part, False), (part, rows - part, True))
    smem = pl.BlockSpec(memory_space=pltpu.SMEM)
    vmem = pl.BlockSpec(memory_space=pltpu.VMEM)
    flops = 2 * rows * cols * cols * narrow
    return pl.pallas_call(
        functools.partial(kernel, narrow, wide, parts),
        out_shape=jax.ShapeDtypeStruct((rows, cols), jnp.float32),
        in_specs=[smem, smem, vmem],
        out_specs=vmem,
        scratch_shapes=[
            pltpu.VMEM((wide, rows, cols), jnp.float32),
            pltpu.VMEM((narrow, rows, cols), jnp.float32),
            pltpu.VMEM((narrow, rows, LANES), jnp.float32),
            pltpu.SemaphoreType.DMA((4, wide, len(parts))),
            pltpu.SemaphoreType.DMA((wide, len(parts))),
            pltpu.SemaphoreType.DMA((narrow,)),
            pltpu.SemaphoreType.DMA((narrow,)),
            pltpu.SemaphoreType.DMA((narrow,)),
            pltpu.SemaphoreType.DMA((narrow,)),
        ],
        compiler_params=pltpu.CompilerParams(
            collective_id=0, has_side_effects=True, vmem_limit_bytes=48 * 1024 * 1024
        ),
        cost_estimate=pl.CostEstimate(flops=flops, bytes_accessed=8 * rows * cols, transcendentals=0),
    )(in_pattern, out_pattern, state)


def solution(mesh):
    return jax.shard_map(
        functools.partial(body, mesh.shape["narrow"], mesh.shape["wide"]),
        mesh=mesh,
        in_specs=(P("wide", "narrow"), P(), P()),
        out_specs=P("wide", "narrow"),
        check_vma=False,
    )
```

```python
import functools

import jax
import jax.numpy as jnp
from jax import lax
from jax.experimental import pallas as pl
from jax.experimental.pallas import tpu as pltpu
from jax.sharding import PartitionSpec as P

BLK = 256
LANES = 128
MESH = pl.DeviceIdType.MESH
UP, DOWN, ACROSS, SIBLING = range(4)


def split(value):
    high = value.astype(jnp.bfloat16)
    low = (value - high.astype(jnp.float32)).astype(jnp.bfloat16)
    return high, low


def kernel(
    narrow, wide, parts, in_hbm, out_hbm, x_hbm, o_ref,
    in_ref, out_pat_ref, blocks, row_parts, left, total, sums, load_sem, send_sem, recv_sem,
    row_send, row_recv, sum_send, sum_recv,
):
    rows, cols = x_hbm.shape
    blks = in_ref.shape[0]
    units = cols // LANES
    line = wide // 4
    group = wide // narrow
    n = lax.axis_index("narrow")
    w = lax.axis_index("wide")
    z, y, c = w // 4, (w // 2) % 2, w % 2

    def index(zz, yy, cc):
        return (zz * 2 + yy) * 2 + cc

    def partner(kind):
        return {
            UP: (n, index(z + 1, y, c)),
            DOWN: (n, index(z - 1, y, c)),
            ACROSS: (n, index(z, 1 - y, c)),
            SIBLING: (n, index(z, y, 1 - c)),
        }[kind]

    loads = [
        pltpu.make_async_copy(source, target, load_sem.at[i])
        for i, (source, target) in enumerate(
            [(x_hbm, blocks.at[w]), (in_hbm, in_ref), (out_hbm, out_pat_ref)]
        )
    ]
    for load in loads:
        load.start()

    has_up, has_down = z + 1 < line, z >= 1
    others = [lax.rem(n + d, narrow) for d in range(1, narrow)]

    barrier = pltpu.get_barrier_semaphore()

    def greet(device):
        pl.semaphore_signal(barrier, inc=1, device_id=device, device_id_type=MESH)

    greet(partner(ACROSS))
    greet(partner(SIBLING))
    for other in others:
        greet((other, w))

    @pl.when(has_up)
    def _():
        greet(partner(UP))

    @pl.when(has_down)
    def _():
        greet(partner(DOWN))

    first = (w * rows) // BLK
    second = jnp.minimum(first + 1, blks - 1)
    upper = lax.broadcasted_iota(jnp.int32, (rows, LANES), 0) < (first + 1) * BLK - w * rows

    def keep(pattern, u):
        col = (n * cols + u * LANES) // BLK
        return jnp.where(
            upper, pattern[first, col].astype(jnp.float32), pattern[second, col].astype(jnp.float32)
        )

    for load in loads:
        load.wait()
    for u in range(units):
        at = slice(u * LANES, (u + 1) * LANES)
        masked = blocks[w, :, at] * keep(in_ref, u)
        blocks[w, :, at] = masked
        row_parts[n, :, at] = masked

    met = 1 + 1 + len(others) + has_up.astype(jnp.int32) + has_down.astype(jnp.int32)
    pl.semaphore_wait(barrier, met)

    def copy(kind, slot, part):
        start, size, _ = parts[part]
        ref = blocks.at[slot, pl.ds(start, size), :]
        return pltpu.make_async_remote_copy(
            src_ref=ref,
            dst_ref=ref,
            send_sem=send_sem.at[kind, slot, part],
            recv_sem=recv_sem.at[slot, part],
            device_id=partner(kind),
            device_id_type=MESH,
        )

    def arrive(slot, part):
        copy(SIBLING, slot, part).wait_recv()

    def go(kind, slot, part, act):
        if kind == UP:
            pl.when(has_up)(lambda: act(copy(kind, slot, part)))
        elif kind == DOWN:
            pl.when(has_down)(lambda: act(copy(kind, slot, part)))
        else:
            act(copy(kind, slot, part))

    def row_copy(other):
        return pltpu.make_async_remote_copy(
            src_ref=blocks.at[w],
            dst_ref=row_parts.at[n],
            send_sem=row_send.at[other],
            recv_sem=row_recv.at[n],
            device_id=(other, w),
            device_id_type=MESH,
        )

    def row_arrival(other):
        return pltpu.make_async_remote_copy(
            src_ref=blocks.at[w],
            dst_ref=row_parts.at[other],
            send_sem=row_send.at[other],
            recv_sem=row_recv.at[other],
            device_id=(other, w),
            device_id_type=MESH,
        )

    count = len(parts)
    across = [p for p in range(count) if parts[p][2]]
    along = [p for p in range(count) if not parts[p][2]]

    def under(condition, act):
        if condition is None:
            act()
        else:
            pl.when(condition)(act)

    def own(visit):
        for part in range(count):
            visit(None, w, part, (UP, DOWN, ACROSS, SIBLING))

    def beside(visit):
        for part in across:
            visit(None, index(z, 1 - y, c), part, (UP, DOWN, SIBLING))
        for part in along:
            visit(None, index(z, 1 - y, c), part, (SIBLING,))

    def along_line(step, visit):
        for part in along:
            visit(z >= step, index(z - step, y, c), part, (UP, ACROSS, SIBLING))
            visit(z + step < line, index(z + step, y, c), part, (DOWN, ACROSS, SIBLING))

    def across_line(step, visit):
        for part in across:
            for yy in (y, 1 - y):
                visit(z >= step, index(z - step, yy, c), part, (UP, SIBLING))
                visit(z + step < line, index(z + step, yy, c), part, (DOWN, SIBLING))
        for part in along:
            visit(z >= step, index(z - step, 1 - y, c), part, (SIBLING,))
            visit(z + step < line, index(z + step, 1 - y, c), part, (SIBLING,))

    def send(condition, slot, part, kinds):
        under(condition, lambda: [go(kind, slot, part, lambda one: one.start()) for kind in kinds] and None)

    def forward(condition, slot, part, kinds):
        def act():
            arrive(slot, part)
            send(None, slot, part, kinds)

        under(condition, act)

    def drain(condition, slot, part, kinds):
        under(condition, lambda: [go(kind, slot, part, lambda one: one.wait_send()) for kind in kinds] and None)

    def multiply(plane):
        for yy in range(2):
            for part in range(count):
                arrive(index(plane, yy, 1 - c), part)
        b_high, b_low = split(blocks[pl.ds(plane * 4, 4)].reshape(4 * rows, cols))
        both = left[plane]
        first_two = jnp.dot(both, b_high, preferred_element_type=jnp.float32)
        term = first_two[:rows] + first_two[rows:]
        total[...] += term + jnp.dot(both[:rows], b_low, preferred_element_type=jnp.float32)

    own(send)
    for other in others:
        row_copy(other).start()
    total[...] = jnp.zeros_like(total)
    beside(forward)

    def prepare():
        for other in others:
            row_arrival(other).wait_recv()
        for g in range(narrow):
            both = jnp.concatenate(split(row_parts[g]), axis=0)
            for q in range(group // 4):
                left[g * (group // 4) + q] = both[:, q * 4 * rows : (q + 1) * 4 * rows]

    def turn(step, carry):
        along_line(step, forward)
        pl.when(step == 1)(prepare)

        def one_side(side, carry):
            plane = z + (2 * side - 1) * (step - 1)
            live = (plane >= 0) & (plane < line) & ((step > 1) | (side == 0))
            pl.when(live)(lambda: multiply(plane))
            return carry

        lax.fori_loop(0, 2, one_side, 0)
        across_line(step, forward)
        return carry

    lax.fori_loop(1, line + 1, turn, 0)

    expanded = total[...]
    partial = None
    for u in range(units):
        at = slice(u * LANES, (u + 1) * LANES)
        inflated = expanded[:, at] * expanded[:, at] * keep(out_pat_ref, u)
        o_ref[:, at] = inflated
        partial = inflated if partial is None else partial + inflated
    sums[n] = partial

    def sum_copy(other, slot):
        return pltpu.make_async_remote_copy(
            src_ref=sums.at[n],
            dst_ref=sums.at[slot],
            send_sem=sum_send.at[other],
            recv_sem=sum_recv.at[slot],
            device_id=(other, w),
            device_id_type=MESH,
        )

    for other in others:
        sum_copy(other, n).start()

    own(drain)
    beside(drain)

    def drain_turn(step, carry):
        along_line(step, drain)
        across_line(step, drain)
        return carry

    lax.fori_loop(1, line, drain_turn, 0)
    for other in others:
        row_copy(other).wait_send()
    for other in others:
        sum_copy(other, other).wait_recv()
    row_sum = sums[0]
    for g in range(1, narrow):
        row_sum = row_sum + sums[g]
    scale = (cols * narrow) / jnp.sum(row_sum, axis=1, keepdims=True)
    o_ref[...] = o_ref[...] * scale
    for other in others:
        sum_copy(other, n).wait_send()


def body(narrow, wide, state, in_pattern, out_pattern):
    rows, cols = state.shape
    cut = 2 * rows // 5
    parts = ((0, cut, False), (cut, cut, False), (2 * cut, rows - 2 * cut, True))
    hbm = pl.BlockSpec(memory_space=pltpu.HBM)
    vmem = pl.BlockSpec(memory_space=pltpu.VMEM)
    flops = 2 * rows * cols * cols * narrow
    return pl.pallas_call(
        functools.partial(kernel, narrow, wide, parts),
        out_shape=jax.ShapeDtypeStruct((rows, cols), jnp.float32),
        in_specs=[hbm, hbm, hbm],
        out_specs=vmem,
        scratch_shapes=[
            pltpu.SMEM(in_pattern.shape, jnp.int32),
            pltpu.SMEM(out_pattern.shape, jnp.int32),
            pltpu.VMEM((wide, rows, cols), jnp.float32),
            pltpu.VMEM((narrow, rows, cols), jnp.float32),
            pltpu.VMEM((wide // 4, 2 * rows, 4 * rows), jnp.bfloat16),
            pltpu.VMEM((rows, cols), jnp.float32),
            pltpu.VMEM((narrow, rows, LANES), jnp.float32),
            pltpu.SemaphoreType.DMA((3,)),
            pltpu.SemaphoreType.DMA((4, wide, len(parts))),
            pltpu.SemaphoreType.DMA((wide, len(parts))),
            pltpu.SemaphoreType.DMA((narrow,)),
            pltpu.SemaphoreType.DMA((narrow,)),
            pltpu.SemaphoreType.DMA((narrow,)),
            pltpu.SemaphoreType.DMA((narrow,)),
        ],
        compiler_params=pltpu.CompilerParams(
            collective_id=0, has_side_effects=True, vmem_limit_bytes=60 * 1024 * 1024
        ),
        cost_estimate=pl.CostEstimate(flops=flops, bytes_accessed=8 * rows * cols, transcendentals=0),
    )(in_pattern, out_pattern, state)


def solution(mesh):
    return jax.shard_map(
        functools.partial(body, mesh.shape["narrow"], mesh.shape["wide"]),
        mesh=mesh,
        in_specs=(P("wide", "narrow"), P(), P()),
        out_specs=P("wide", "narrow"),
        check_vma=False,
    )
```

```python
import functools

import jax
import jax.numpy as jnp
from jax import lax
from jax.experimental import pallas as pl
from jax.experimental.pallas import tpu as pltpu
from jax.sharding import PartitionSpec as P

BLK = 256
LANES = 128
MESH = pl.DeviceIdType.MESH
UP, DOWN, ACROSS, SIBLING = range(4)
LINE = UP


def split(value):
    high = value.astype(jnp.bfloat16)
    low = (value - high.astype(jnp.float32)).astype(jnp.bfloat16)
    return high, low


def kernel(
    narrow, wide, cut, in_hbm, out_hbm, x_hbm, o_ref,
    in_ref, out_pat_ref, blocks, row_parts, left, total, sums, load_sem, send_sem, recv_sem,
    row_send, row_recv, sum_send, sum_recv,
):
    rows, cols = x_hbm.shape
    blks = in_ref.shape[0]
    units = cols // LANES
    line = wide // 4
    group = wide // narrow
    n = lax.axis_index("narrow")
    w = lax.axis_index("wide")
    z, y, c = w // 4, (w // 2) % 2, w % 2

    def index(zz, yy, cc):
        return (zz * 2 + yy) * 2 + cc

    def partner(kind):
        return {
            UP: (n, index(z + 1, y, c)),
            DOWN: (n, index(z - 1, y, c)),
            ACROSS: (n, index(z, 1 - y, c)),
            SIBLING: (n, index(z, y, 1 - c)),
        }[kind]

    loads = [
        pltpu.make_async_copy(source, target, load_sem.at[i])
        for i, (source, target) in enumerate(
            [(x_hbm, blocks.at[c, z, y]), (in_hbm, in_ref), (out_hbm, out_pat_ref)]
        )
    ]
    for load in loads:
        load.start()

    has_up, has_down = z + 1 < line, z >= 1
    others = [lax.rem(n + d, narrow) for d in range(1, narrow)]

    barrier = pltpu.get_barrier_semaphore()

    def greet(device):
        pl.semaphore_signal(barrier, inc=1, device_id=device, device_id_type=MESH)

    greet(partner(ACROSS))
    greet(partner(SIBLING))
    for other in others:
        greet((other, w))

    @pl.when(has_up)
    def _():
        greet(partner(UP))

    @pl.when(has_down)
    def _():
        greet(partner(DOWN))

    first = (w * rows) // BLK
    second = jnp.minimum(first + 1, blks - 1)
    upper = lax.broadcasted_iota(jnp.int32, (rows, LANES), 0) < (first + 1) * BLK - w * rows

    def keep(pattern, u):
        col = (n * cols + u * LANES) // BLK
        return jnp.where(
            upper, pattern[first, col].astype(jnp.float32), pattern[second, col].astype(jnp.float32)
        )

    for load in loads:
        load.wait()
    for u in range(units):
        at = slice(u * LANES, (u + 1) * LANES)
        masked = blocks[c, z, y, :, at] * keep(in_ref, u)
        blocks[c, z, y, :, at] = masked
        row_parts[n, :, at] = masked

    met = 1 + 1 + len(others) + has_up.astype(jnp.int32) + has_down.astype(jnp.int32)
    pl.semaphore_wait(barrier, met)

    low, rest = pl.ds(0, 2 * cut), pl.ds(2 * cut, rows - 2 * cut)

    def piece(core, plane, yy, part):
        return blocks.at[core, plane, yy, pl.ds(part * cut, cut), :]

    def both_rest(core, plane):
        return blocks.at[core, plane, :, rest, :]

    def copy(kind, ref, plane, number):
        via = {UP: 0, DOWN: 0, ACROSS: 1, SIBLING: 2}[kind]
        return pltpu.make_async_remote_copy(
            src_ref=ref,
            dst_ref=ref,
            send_sem=send_sem.at[kind, plane, number],
            recv_sem=recv_sem.at[via, plane, number],
            device_id=partner(kind),
            device_id_type=MESH,
        )

    def start(kind, ref, plane, number):
        one = copy(kind, ref, plane, number)
        if kind == UP:
            pl.when(has_up)(one.start)
        elif kind == DOWN:
            pl.when(has_down)(one.start)
        else:
            one.start()

    def finish(kind, ref, plane, number):
        one = copy(kind, ref, plane, number)
        if kind == UP:
            pl.when(has_up)(one.wait_send)
        elif kind == DOWN:
            pl.when(has_down)(one.wait_send)
        else:
            one.wait_send()

    def arrive(kind, ref, plane, number):
        copy(kind, ref, plane, number).wait_recv()

    def nothing(*_):
        pass

    def row_copy(other):
        return pltpu.make_async_remote_copy(
            src_ref=blocks.at[c, z, y],
            dst_ref=row_parts.at[n],
            send_sem=row_send.at[other],
            recv_sem=row_recv.at[n],
            device_id=(other, w),
            device_id_type=MESH,
        )

    def row_arrival(other):
        return pltpu.make_async_remote_copy(
            src_ref=blocks.at[c, z, y],
            dst_ref=row_parts.at[other],
            send_sem=row_send.at[other],
            recv_sem=row_recv.at[other],
            device_id=(other, w),
            device_id_type=MESH,
        )

    def own(act):
        for part in range(2):
            ref = piece(c, z, y, part)
            for kind in (UP, DOWN, ACROSS):
                act(kind, ref, z, part)
        act(ACROSS, blocks.at[c, z, y, rest, :], z, 2)
        act(SIBLING, blocks.at[c, z, y, low, :], z, 0)

    def beside(wait, act):
        wait(ACROSS, blocks.at[c, z, 1 - y, rest, :], z, 2)
        for kind in (UP, DOWN, SIBLING):
            act(kind, both_rest(c, z), z, 2)
        from_across(z, wait, act)

    def from_across(plane, wait, act):
        for part in range(2):
            wait(ACROSS, piece(c, plane, 1 - y, part), plane, part)
        act(SIBLING, blocks.at[c, plane, 1 - y, low, :], plane, 1)

    def sides(step, visit):
        pl.when(z >= step)(lambda: visit(z - step, UP))
        pl.when(z + step < line)(lambda: visit(z + step, DOWN))

    def along_line(step, wait, act):
        for part in range(2):

            def one_piece(plane, kind):
                ref = piece(c, plane, y, part)
                wait(LINE, ref, plane, part)
                act(kind, ref, plane, part)
                act(ACROSS, ref, plane, part)
                if part == 1:
                    act(SIBLING, blocks.at[c, plane, y, low, :], plane, 0)

            sides(step, one_piece)

    def rest_of_line(step, wait, act):
        def the_rest(plane, kind):
            ref = both_rest(c, plane)
            wait(LINE, ref, plane, 2)
            act(kind, ref, plane, 2)
            act(SIBLING, ref, plane, 2)

        sides(step, the_rest)
        sides(step, lambda plane, kind: from_across(plane, wait, act))

    def half(plane, core):
        b_high, b_low = split(blocks[core, plane].reshape(2 * rows, cols))
        pair = left[plane, core]
        first_two = jnp.dot(pair, b_high, preferred_element_type=jnp.float32)
        term = first_two[:rows] + first_two[rows:]
        total[...] += term + jnp.dot(pair[:rows], b_low, preferred_element_type=jnp.float32)

    def multiply(plane):
        def one_half(h, carry):
            @pl.when(h == 1)
            def _():
                arrive(SIBLING, blocks.at[1 - c, plane, y, low, :], plane, 0)
                arrive(SIBLING, blocks.at[1 - c, plane, 1 - y, low, :], plane, 1)
                arrive(SIBLING, both_rest(1 - c, plane), plane, 2)

            half(plane, (c + h) % 2)
            return carry

        lax.fori_loop(0, 2, one_half, 0)

    own(start)
    for other in others:
        row_copy(other).start()
    total[...] = jnp.zeros_like(total)
    beside(arrive, start)

    def prepare():
        for other in others:
            row_arrival(other).wait_recv()
        for g in range(narrow):
            both = jnp.concatenate(split(row_parts[g]), axis=0)
            for q in range(group // 4):
                for core in range(2):
                    begins = [(q * 4 + 2 * yy + core) * rows for yy in range(2)]
                    left[g * (group // 4) + q, core] = jnp.concatenate(
                        [both[:, begin : begin + rows] for begin in begins], axis=1
                    )

    def turn(step, carry):
        along_line(step, arrive, start)
        pl.when(step == 1)(prepare)

        def one_side(side, carry):
            plane = z + (2 * side - 1) * (step - 1)
            live = (plane >= 0) & (plane < line) & ((step > 1) | (side == 0))
            pl.when(live)(lambda: multiply(plane))
            return carry

        lax.fori_loop(0, 2, one_side, 0)
        rest_of_line(step, arrive, start)
        return carry

    lax.fori_loop(1, line + 1, turn, 0)

    expanded = total[...]
    partial = None
    for u in range(units):
        at = slice(u * LANES, (u + 1) * LANES)
        inflated = expanded[:, at] * expanded[:, at] * keep(out_pat_ref, u)
        o_ref[:, at] = inflated
        partial = inflated if partial is None else partial + inflated
    sums[n] = partial

    def sum_copy(other, slot):
        return pltpu.make_async_remote_copy(
            src_ref=sums.at[n],
            dst_ref=sums.at[slot],
            send_sem=sum_send.at[other],
            recv_sem=sum_recv.at[slot],
            device_id=(other, w),
            device_id_type=MESH,
        )

    for other in others:
        sum_copy(other, n).start()

    own(finish)
    beside(nothing, finish)

    def drain_turn(step, carry):
        along_line(step, nothing, finish)
        rest_of_line(step, nothing, finish)
        return carry

    lax.fori_loop(1, line, drain_turn, 0)
    for other in others:
        row_copy(other).wait_send()
    for other in others:
        sum_copy(other, other).wait_recv()
    row_sum = sums[0]
    for g in range(1, narrow):
        row_sum = row_sum + sums[g]
    scale = (cols * narrow) / jnp.sum(row_sum, axis=1, keepdims=True)
    o_ref[...] = o_ref[...] * scale
    for other in others:
        sum_copy(other, n).wait_send()


def body(narrow, wide, state, in_pattern, out_pattern):
    rows, cols = state.shape
    cut = 2 * rows // 5
    line = wide // 4
    hbm = pl.BlockSpec(memory_space=pltpu.HBM)
    vmem = pl.BlockSpec(memory_space=pltpu.VMEM)
    flops = 2 * rows * cols * cols * narrow
    return pl.pallas_call(
        functools.partial(kernel, narrow, wide, cut),
        out_shape=pltpu.VMEM((rows, cols), jnp.float32),
        in_specs=[hbm, hbm, hbm],
        out_specs=vmem,
        scratch_shapes=[
            pltpu.SMEM(in_pattern.shape, jnp.int32),
            pltpu.SMEM(out_pattern.shape, jnp.int32),
            pltpu.VMEM((2, line, 2, rows, cols), jnp.float32),
            pltpu.VMEM((narrow, rows, cols), jnp.float32),
            pltpu.VMEM((line, 2, 2 * rows, 2 * rows), jnp.bfloat16),
            pltpu.VMEM((rows, cols), jnp.float32),
            pltpu.VMEM((narrow, rows, LANES), jnp.float32),
            pltpu.SemaphoreType.DMA((3,)),
            pltpu.SemaphoreType.DMA((4, line, 3)),
            pltpu.SemaphoreType.DMA((3, line, 3)),
            pltpu.SemaphoreType.DMA((narrow,)),
            pltpu.SemaphoreType.DMA((narrow,)),
            pltpu.SemaphoreType.DMA((narrow,)),
            pltpu.SemaphoreType.DMA((narrow,)),
        ],
        compiler_params=pltpu.CompilerParams(
            collective_id=0, has_side_effects=True, vmem_limit_bytes=48 * 1024 * 1024
        ),
        cost_estimate=pl.CostEstimate(flops=flops, bytes_accessed=8 * rows * cols, transcendentals=0),
    )(*[pltpu.with_memory_space_constraint(a, pltpu.HBM) for a in (in_pattern, out_pattern, state)])


def solution(mesh):
    return jax.shard_map(
        functools.partial(body, mesh.shape["narrow"], mesh.shape["wide"]),
        mesh=mesh,
        in_specs=(P("wide", "narrow"), P(), P()),
        out_specs=P("wide", "narrow"),
        check_vma=False,
    )
```

```python
import functools

import jax
import jax.numpy as jnp
from jax import lax
from jax.experimental import pallas as pl
from jax.experimental.pallas import tpu as pltpu
from jax.sharding import PartitionSpec as P

BLK = 256
LANES = 128
MESH = pl.DeviceIdType.MESH
UP, DOWN, ACROSS, SIBLING = range(4)
LINE = UP


def split(value):
    high = value.astype(jnp.bfloat16)
    low = (value - high.astype(jnp.float32)).astype(jnp.bfloat16)
    return high, low


def kernel(
    narrow, wide, cut, in_hbm, out_hbm, x_hbm, o_ref,
    in_ref, out_pat_ref, blocks, row_parts, left, total, sums, load_sem, send_sem, recv_sem,
    row_send, row_recv, sum_send, sum_recv,
):
    rows, cols = x_hbm.shape
    blks = in_ref.shape[0]
    units = cols // LANES
    line = wide // 4
    group = wide // narrow
    n = lax.axis_index("narrow")
    w = lax.axis_index("wide")
    z, y, c = w // 4, (w // 2) % 2, w % 2

    def index(zz, yy, cc):
        return (zz * 2 + yy) * 2 + cc

    def partner(kind):
        return {
            UP: (n, index(z + 1, y, c)),
            DOWN: (n, index(z - 1, y, c)),
            ACROSS: (n, index(z, 1 - y, c)),
            SIBLING: (n, index(z, y, 1 - c)),
        }[kind]

    loads = [
        pltpu.make_async_copy(source, target, load_sem.at[i])
        for i, (source, target) in enumerate(
            [(x_hbm, blocks.at[c, z, y]), (in_hbm, in_ref), (out_hbm, out_pat_ref)]
        )
    ]
    for load in loads:
        load.start()

    has_up, has_down = z + 1 < line, z >= 1
    others = [lax.rem(n + d, narrow) for d in range(1, narrow)]

    barrier = pltpu.get_barrier_semaphore()

    def greet(device):
        pl.semaphore_signal(barrier, inc=1, device_id=device, device_id_type=MESH)

    greet(partner(ACROSS))
    greet(partner(SIBLING))
    for other in others:
        greet((other, w))

    @pl.when(has_up)
    def _():
        greet(partner(UP))

    @pl.when(has_down)
    def _():
        greet(partner(DOWN))

    first = (w * rows) // BLK
    second = jnp.minimum(first + 1, blks - 1)
    upper = lax.broadcasted_iota(jnp.int32, (rows, LANES), 0) < (first + 1) * BLK - w * rows

    def keep(pattern, u):
        col = (n * cols + u * LANES) // BLK
        return jnp.where(
            upper, pattern[first, col].astype(jnp.float32), pattern[second, col].astype(jnp.float32)
        )

    for load in loads:
        load.wait()
    for u in range(units):
        at = slice(u * LANES, (u + 1) * LANES)
        masked = blocks[c, z, y, :, at] * keep(in_ref, u)
        blocks[c, z, y, :, at] = masked
        row_parts[n, :, at] = masked

    met = 1 + 1 + len(others) + has_up.astype(jnp.int32) + has_down.astype(jnp.int32)
    pl.semaphore_wait(barrier, met)

    low, rest = pl.ds(0, 2 * cut), pl.ds(2 * cut, rows - 2 * cut)

    def piece(core, plane, yy, part):
        return blocks.at[core, plane, yy, pl.ds(part * cut, cut), :]

    def both_rest(core, plane):
        return blocks.at[core, plane, :, rest, :]

    def copy(kind, ref, plane, number):
        via = {UP: 0, DOWN: 0, ACROSS: 1, SIBLING: 2}[kind]
        return pltpu.make_async_remote_copy(
            src_ref=ref,
            dst_ref=ref,
            send_sem=send_sem.at[kind, plane, number],
            recv_sem=recv_sem.at[via, plane, number],
            device_id=partner(kind),
            device_id_type=MESH,
        )

    def start(kind, ref, plane, number):
        one = copy(kind, ref, plane, number)
        if kind == UP:
            pl.when(has_up)(one.start)
        elif kind == DOWN:
            pl.when(has_down)(one.start)
        else:
            one.start()

    def finish(kind, ref, plane, number):
        one = copy(kind, ref, plane, number)
        if kind == UP:
            pl.when(has_up)(one.wait_send)
        elif kind == DOWN:
            pl.when(has_down)(one.wait_send)
        else:
            one.wait_send()

    def arrive(kind, ref, plane, number):
        copy(kind, ref, plane, number).wait_recv()

    def nothing(*_):
        pass

    def row_copy(other):
        return pltpu.make_async_remote_copy(
            src_ref=blocks.at[c, z, y],
            dst_ref=row_parts.at[n],
            send_sem=row_send.at[other],
            recv_sem=row_recv.at[n],
            device_id=(other, w),
            device_id_type=MESH,
        )

    def row_arrival(other):
        return pltpu.make_async_remote_copy(
            src_ref=blocks.at[c, z, y],
            dst_ref=row_parts.at[other],
            send_sem=row_send.at[other],
            recv_sem=row_recv.at[other],
            device_id=(other, w),
            device_id_type=MESH,
        )

    def own(act):
        act(ACROSS, blocks.at[c, z, y, rest, :], z, 2)
        for part in range(2):
            ref = piece(c, z, y, part)
            for kind in (UP, DOWN, ACROSS):
                act(kind, ref, z, part)
        act(SIBLING, blocks.at[c, z, y, low, :], z, 0)

    def beside(wait, act):
        wait(ACROSS, blocks.at[c, z, 1 - y, rest, :], z, 2)
        for kind in (UP, DOWN, SIBLING):
            act(kind, both_rest(c, z), z, 2)

    def from_across(plane, wait, act):
        for part in range(2):
            wait(ACROSS, piece(c, plane, 1 - y, part), plane, part)
        act(SIBLING, blocks.at[c, plane, 1 - y, low, :], plane, 1)

    def sides(step, visit):
        pl.when(z >= step)(lambda: visit(z - step, UP))
        pl.when(z + step < line)(lambda: visit(z + step, DOWN))

    def along_line(step, wait, act):
        for part in range(2):

            def one_piece(plane, kind):
                ref = piece(c, plane, y, part)
                wait(LINE, ref, plane, part)
                act(kind, ref, plane, part)
                act(ACROSS, ref, plane, part)
                if part == 1:
                    act(SIBLING, blocks.at[c, plane, y, low, :], plane, 0)

            sides(step, one_piece)

    def rest_of_line(step, wait, act):
        def the_rest(plane, kind):
            ref = both_rest(c, plane)
            wait(LINE, ref, plane, 2)
            act(kind, ref, plane, 2)
            act(SIBLING, ref, plane, 2)

        sides(step, the_rest)
        sides(step, lambda plane, kind: from_across(plane, wait, act))

    def half(plane, core):
        b_high, b_low = split(blocks[core, plane].reshape(2 * rows, cols))
        pair = left[plane, core]
        first_two = jnp.dot(pair, b_high, preferred_element_type=jnp.float32)
        term = first_two[:rows] + first_two[rows:]
        total[...] += term + jnp.dot(pair[:rows], b_low, preferred_element_type=jnp.float32)

    def multiply(plane):
        def one_half(h, carry):
            @pl.when(h == 1)
            def _():
                arrive(SIBLING, blocks.at[1 - c, plane, y, low, :], plane, 0)
                arrive(SIBLING, blocks.at[1 - c, plane, 1 - y, low, :], plane, 1)
                arrive(SIBLING, both_rest(1 - c, plane), plane, 2)

            half(plane, (c + h) % 2)
            return carry

        lax.fori_loop(0, 2, one_half, 0)

    own(start)
    for other in others:
        row_copy(other).start()
    total[...] = jnp.zeros_like(total)
    beside(arrive, start)

    def prepare():
        for other in others:
            row_arrival(other).wait_recv()
        for g in range(narrow):
            both = jnp.concatenate(split(row_parts[g]), axis=0)
            for q in range(group // 4):
                for core in range(2):
                    begins = [(q * 4 + 2 * yy + core) * rows for yy in range(2)]
                    left[g * (group // 4) + q, core] = jnp.concatenate(
                        [both[:, begin : begin + rows] for begin in begins], axis=1
                    )

    def turn(step, carry):
        along_line(step, arrive, start)

        @pl.when(step == 1)
        def _():
            from_across(z, arrive, start)
            prepare()

        def one_side(side, carry):
            plane = z + (2 * side - 1) * (step - 1)
            live = (plane >= 0) & (plane < line) & ((step > 1) | (side == 0))
            pl.when(live)(lambda: multiply(plane))
            return carry

        lax.fori_loop(0, 2, one_side, 0)
        rest_of_line(step, arrive, start)
        return carry

    lax.fori_loop(1, line + 1, turn, 0)

    expanded = total[...]
    partial = None
    for u in range(units):
        at = slice(u * LANES, (u + 1) * LANES)
        inflated = expanded[:, at] * expanded[:, at] * keep(out_pat_ref, u)
        o_ref[:, at] = inflated
        partial = inflated if partial is None else partial + inflated
    sums[n] = partial

    def sum_copy(other, slot):
        return pltpu.make_async_remote_copy(
            src_ref=sums.at[n],
            dst_ref=sums.at[slot],
            send_sem=sum_send.at[other],
            recv_sem=sum_recv.at[slot],
            device_id=(other, w),
            device_id_type=MESH,
        )

    for other in others:
        sum_copy(other, n).start()

    own(finish)
    beside(nothing, finish)
    from_across(z, nothing, finish)

    def drain_turn(step, carry):
        along_line(step, nothing, finish)
        rest_of_line(step, nothing, finish)
        return carry

    lax.fori_loop(1, line, drain_turn, 0)
    for other in others:
        row_copy(other).wait_send()
    for other in others:
        sum_copy(other, other).wait_recv()
    row_sum = sums[0]
    for g in range(1, narrow):
        row_sum = row_sum + sums[g]
    scale = (cols * narrow) / jnp.sum(row_sum, axis=1, keepdims=True)
    o_ref[...] = o_ref[...] * scale
    for other in others:
        sum_copy(other, n).wait_send()


def body(narrow, wide, state, in_pattern, out_pattern):
    rows, cols = state.shape
    cut = 2 * rows // 5
    line = wide // 4
    hbm = pl.BlockSpec(memory_space=pltpu.HBM)
    vmem = pl.BlockSpec(memory_space=pltpu.VMEM)
    flops = 2 * rows * cols * cols * narrow
    return pl.pallas_call(
        functools.partial(kernel, narrow, wide, cut),
        out_shape=pltpu.VMEM((rows, cols), jnp.float32),
        in_specs=[hbm, hbm, hbm],
        out_specs=vmem,
        scratch_shapes=[
            pltpu.SMEM(in_pattern.shape, jnp.int32),
            pltpu.SMEM(out_pattern.shape, jnp.int32),
            pltpu.VMEM((2, line, 2, rows, cols), jnp.float32),
            pltpu.VMEM((narrow, rows, cols), jnp.float32),
            pltpu.VMEM((line, 2, 2 * rows, 2 * rows), jnp.bfloat16),
            pltpu.VMEM((rows, cols), jnp.float32),
            pltpu.VMEM((narrow, rows, LANES), jnp.float32),
            pltpu.SemaphoreType.DMA((3,)),
            pltpu.SemaphoreType.DMA((4, line, 3)),
            pltpu.SemaphoreType.DMA((3, line, 3)),
            pltpu.SemaphoreType.DMA((narrow,)),
            pltpu.SemaphoreType.DMA((narrow,)),
            pltpu.SemaphoreType.DMA((narrow,)),
            pltpu.SemaphoreType.DMA((narrow,)),
        ],
        compiler_params=pltpu.CompilerParams(
            collective_id=0, has_side_effects=True, vmem_limit_bytes=48 * 1024 * 1024
        ),
        cost_estimate=pl.CostEstimate(flops=flops, bytes_accessed=8 * rows * cols, transcendentals=0),
    )(*[pltpu.with_memory_space_constraint(a, pltpu.HBM) for a in (in_pattern, out_pattern, state)])


def solution(mesh):
    return jax.shard_map(
        functools.partial(body, mesh.shape["narrow"], mesh.shape["wide"]),
        mesh=mesh,
        in_specs=(P("wide", "narrow"), P(), P()),
        out_specs=P("wide", "narrow"),
        check_vma=False,
    )
```

```python
import functools

import jax
import jax.numpy as jnp
from jax import lax
from jax.experimental import pallas as pl
from jax.experimental.pallas import tpu as pltpu
from jax.sharding import PartitionSpec as P

BLK = 256
LANES = 128
MESH = pl.DeviceIdType.MESH
UP, DOWN, ACROSS, SIBLING = range(4)
LINE = UP


def split(value):
    high = value.astype(jnp.bfloat16)
    low = (value - high.astype(jnp.float32)).astype(jnp.bfloat16)
    return high, low


def kernel(
    narrow, wide, cut, in_hbm, out_hbm, x_hbm, o_ref,
    in_ref, out_pat_ref, blocks, row_parts, left, total, sums, load_sem, send_sem, recv_sem,
    row_send, row_recv, sum_send, sum_recv,
):
    rows, cols = x_hbm.shape
    blks = in_ref.shape[0]
    units = cols // LANES
    line = wide // 4
    group = wide // narrow
    n = lax.axis_index("narrow")
    w = lax.axis_index("wide")
    z, y, c = w // 4, (w // 2) % 2, w % 2

    def index(zz, yy, cc):
        return (zz * 2 + yy) * 2 + cc

    def partner(kind):
        return {
            UP: (n, index(z + 1, y, c)),
            DOWN: (n, index(z - 1, y, c)),
            ACROSS: (n, index(z, 1 - y, c)),
            SIBLING: (n, index(z, y, 1 - c)),
        }[kind]

    loads = [
        pltpu.make_async_copy(source, target, load_sem.at[i])
        for i, (source, target) in enumerate(
            [(x_hbm, blocks.at[c, z, y]), (in_hbm, in_ref), (out_hbm, out_pat_ref)]
        )
    ]
    for load in loads:
        load.start()

    has_up, has_down = z + 1 < line, z >= 1
    others = [lax.rem(n + d, narrow) for d in range(1, narrow)]

    barrier = pltpu.get_barrier_semaphore()

    def greet(device):
        pl.semaphore_signal(barrier, inc=1, device_id=device, device_id_type=MESH)

    greet(partner(ACROSS))
    greet(partner(SIBLING))
    for other in others:
        greet((other, w))

    @pl.when(has_up)
    def _():
        greet(partner(UP))

    @pl.when(has_down)
    def _():
        greet(partner(DOWN))

    first = (w * rows) // BLK
    second = jnp.minimum(first + 1, blks - 1)
    upper = lax.broadcasted_iota(jnp.int32, (rows, LANES), 0) < (first + 1) * BLK - w * rows

    def keep(pattern, u):
        col = (n * cols + u * LANES) // BLK
        return jnp.where(
            upper, pattern[first, col].astype(jnp.float32), pattern[second, col].astype(jnp.float32)
        )

    for load in loads:
        load.wait()
    for u in range(units):
        at = slice(u * LANES, (u + 1) * LANES)
        masked = blocks[c, z, y, :, at] * keep(in_ref, u)
        blocks[c, z, y, :, at] = masked
        row_parts[n, :, at] = masked

    met = 1 + 1 + len(others) + has_up.astype(jnp.int32) + has_down.astype(jnp.int32)
    pl.semaphore_wait(barrier, met)

    low, rest = pl.ds(0, 2 * cut), pl.ds(2 * cut, rows - 2 * cut)

    def piece(core, plane, yy, part):
        return blocks.at[core, plane, yy, pl.ds(part * cut, cut), :]

    def both_rest(core, plane):
        return blocks.at[core, plane, :, rest, :]

    def copy(kind, ref, plane, number):
        via = {UP: 0, DOWN: 0, ACROSS: 1, SIBLING: 2}[kind]
        return pltpu.make_async_remote_copy(
            src_ref=ref,
            dst_ref=ref,
            send_sem=send_sem.at[kind, plane, number],
            recv_sem=recv_sem.at[via, plane, number],
            device_id=partner(kind),
            device_id_type=MESH,
        )

    def start(kind, ref, plane, number):
        one = copy(kind, ref, plane, number)
        if kind == UP:
            pl.when(has_up)(one.start)
        elif kind == DOWN:
            pl.when(has_down)(one.start)
        else:
            one.start()

    def finish(kind, ref, plane, number):
        one = copy(kind, ref, plane, number)
        if kind == UP:
            pl.when(has_up)(one.wait_send)
        elif kind == DOWN:
            pl.when(has_down)(one.wait_send)
        else:
            one.wait_send()

    def arrive(kind, ref, plane, number):
        copy(kind, ref, plane, number).wait_recv()

    def nothing(*_):
        pass

    def row_copy(other):
        return pltpu.make_async_remote_copy(
            src_ref=blocks.at[c, z, y],
            dst_ref=row_parts.at[n],
            send_sem=row_send.at[other],
            recv_sem=row_recv.at[n],
            device_id=(other, w),
            device_id_type=MESH,
        )

    def row_arrival(other):
        return pltpu.make_async_remote_copy(
            src_ref=blocks.at[c, z, y],
            dst_ref=row_parts.at[other],
            send_sem=row_send.at[other],
            recv_sem=row_recv.at[other],
            device_id=(other, w),
            device_id_type=MESH,
        )

    def own(act):
        act(ACROSS, blocks.at[c, z, y, rest, :], z, 2)
        for part in range(2):
            ref = piece(c, z, y, part)
            for kind in (UP, DOWN, ACROSS):
                act(kind, ref, z, part)
        act(SIBLING, blocks.at[c, z, y, low, :], z, 0)

    def beside(wait, act):
        wait(ACROSS, blocks.at[c, z, 1 - y, rest, :], z, 2)
        for kind in (UP, DOWN, SIBLING):
            act(kind, both_rest(c, z), z, 2)

    def from_across(plane, wait, act):
        for part in range(2):
            wait(ACROSS, piece(c, plane, 1 - y, part), plane, part)
        act(SIBLING, blocks.at[c, plane, 1 - y, low, :], plane, 1)

    def sides(step, visit):
        pl.when(z >= step)(lambda: visit(z - step, UP))
        pl.when(z + step < line)(lambda: visit(z + step, DOWN))

    def along_line(step, wait, act):
        for part in range(2):

            def one_piece(plane, kind):
                ref = piece(c, plane, y, part)
                wait(LINE, ref, plane, part)
                act(kind, ref, plane, part)
                act(ACROSS, ref, plane, part)
                if part == 1:
                    act(SIBLING, blocks.at[c, plane, y, low, :], plane, 0)

            sides(step, one_piece)

    def rest_of_line(step, wait, act):
        def the_rest(plane, kind):
            ref = both_rest(c, plane)
            wait(LINE, ref, plane, 2)
            act(kind, ref, plane, 2)
            act(SIBLING, ref, plane, 2)

        sides(step, the_rest)

    def half(plane, core):
        b_high, b_low = split(blocks[core, plane].reshape(2 * rows, cols))
        pair = left[plane, core]
        first_two = jnp.dot(pair, b_high, preferred_element_type=jnp.float32)
        term = first_two[:rows] + first_two[rows:]
        total[...] += term + jnp.dot(pair[:rows], b_low, preferred_element_type=jnp.float32)

    def multiply(plane):
        def one_half(h, carry):
            @pl.when(h == 1)
            def _():
                arrive(SIBLING, blocks.at[1 - c, plane, y, low, :], plane, 0)
                arrive(SIBLING, blocks.at[1 - c, plane, 1 - y, low, :], plane, 1)
                arrive(SIBLING, both_rest(1 - c, plane), plane, 2)

            half(plane, (c + h) % 2)
            return carry

        lax.fori_loop(0, 2, one_half, 0)

    own(start)
    for other in others:
        row_copy(other).start()
    total[...] = jnp.zeros_like(total)
    beside(arrive, start)

    def prepare():
        for other in others:
            row_arrival(other).wait_recv()
        for g in range(narrow):
            both = jnp.concatenate(split(row_parts[g]), axis=0)
            for q in range(group // 4):
                for core in range(2):
                    begins = [(q * 4 + 2 * yy + core) * rows for yy in range(2)]
                    left[g * (group // 4) + q, core] = jnp.concatenate(
                        [both[:, begin : begin + rows] for begin in begins], axis=1
                    )

    def late(step):
        @pl.when(step == 0)
        def _():
            from_across(z, arrive, start)
            prepare()

        @pl.when(step > 0)
        def _():
            sides(step, lambda plane, kind: from_across(plane, arrive, start))

        def one_side(side, carry):
            plane = z + (2 * side - 1) * step
            live = (plane >= 0) & (plane < line) & ((step > 0) | (side == 0))
            pl.when(live)(lambda: multiply(plane))
            return carry

        lax.fori_loop(0, 2, one_side, 0)

    at_end = (z == 0) | (z == line - 1)

    def turn(step, carry):
        along_line(step, arrive, start)
        pl.when(at_end)(lambda: late(step - 1))
        rest_of_line(step, arrive, start)
        pl.when(jnp.logical_not(at_end))(lambda: late(step - 1))
        return carry

    lax.fori_loop(1, line + 1, turn, 0)

    expanded = total[...]
    partial = None
    for u in range(units):
        at = slice(u * LANES, (u + 1) * LANES)
        inflated = expanded[:, at] * expanded[:, at] * keep(out_pat_ref, u)
        o_ref[:, at] = inflated
        partial = inflated if partial is None else partial + inflated
    sums[n] = partial

    def sum_copy(other, slot):
        return pltpu.make_async_remote_copy(
            src_ref=sums.at[n],
            dst_ref=sums.at[slot],
            send_sem=sum_send.at[other],
            recv_sem=sum_recv.at[slot],
            device_id=(other, w),
            device_id_type=MESH,
        )

    for other in others:
        sum_copy(other, n).start()

    own(finish)
    beside(nothing, finish)
    from_across(z, nothing, finish)

    def drain_turn(step, carry):
        along_line(step, nothing, finish)
        rest_of_line(step, nothing, finish)
        sides(step, lambda plane, kind: from_across(plane, nothing, finish))
        return carry

    lax.fori_loop(1, line, drain_turn, 0)
    for other in others:
        row_copy(other).wait_send()
    for other in others:
        sum_copy(other, other).wait_recv()
    row_sum = sums[0]
    for g in range(1, narrow):
        row_sum = row_sum + sums[g]
    scale = (cols * narrow) / jnp.sum(row_sum, axis=1, keepdims=True)
    o_ref[...] = o_ref[...] * scale
    for other in others:
        sum_copy(other, n).wait_send()


def body(narrow, wide, state, in_pattern, out_pattern):
    rows, cols = state.shape
    cut = 2 * rows // 5
    line = wide // 4
    hbm = pl.BlockSpec(memory_space=pltpu.HBM)
    vmem = pl.BlockSpec(memory_space=pltpu.VMEM)
    flops = 2 * rows * cols * cols * narrow
    return pl.pallas_call(
        functools.partial(kernel, narrow, wide, cut),
        out_shape=pltpu.VMEM((rows, cols), jnp.float32),
        in_specs=[hbm, hbm, hbm],
        out_specs=vmem,
        scratch_shapes=[
            pltpu.SMEM(in_pattern.shape, jnp.int32),
            pltpu.SMEM(out_pattern.shape, jnp.int32),
            pltpu.VMEM((2, line, 2, rows, cols), jnp.float32),
            pltpu.VMEM((narrow, rows, cols), jnp.float32),
            pltpu.VMEM((line, 2, 2 * rows, 2 * rows), jnp.bfloat16),
            pltpu.VMEM((rows, cols), jnp.float32),
            pltpu.VMEM((narrow, rows, LANES), jnp.float32),
            pltpu.SemaphoreType.DMA((3,)),
            pltpu.SemaphoreType.DMA((4, line, 3)),
            pltpu.SemaphoreType.DMA((3, line, 3)),
            pltpu.SemaphoreType.DMA((narrow,)),
            pltpu.SemaphoreType.DMA((narrow,)),
            pltpu.SemaphoreType.DMA((narrow,)),
            pltpu.SemaphoreType.DMA((narrow,)),
        ],
        compiler_params=pltpu.CompilerParams(
            collective_id=0, has_side_effects=True, vmem_limit_bytes=48 * 1024 * 1024
        ),
        cost_estimate=pl.CostEstimate(flops=flops, bytes_accessed=8 * rows * cols, transcendentals=0),
    )(*[pltpu.with_memory_space_constraint(a, pltpu.HBM) for a in (in_pattern, out_pattern, state)])


def solution(mesh):
    return jax.shard_map(
        functools.partial(body, mesh.shape["narrow"], mesh.shape["wide"]),
        mesh=mesh,
        in_specs=(P("wide", "narrow"), P(), P()),
        out_specs=P("wide", "narrow"),
        check_vma=False,
    )
```

```python
import functools

import jax
import jax.numpy as jnp
from jax import lax
from jax.experimental import pallas as pl
from jax.experimental.pallas import tpu as pltpu
from jax.sharding import PartitionSpec as P

BLK = 256
LANES = 128
MESH = pl.DeviceIdType.MESH
UP, DOWN, ACROSS, SIBLING = range(4)
LINE = UP


def split(value):
    high = value.astype(jnp.bfloat16)
    low = (value - high.astype(jnp.float32)).astype(jnp.bfloat16)
    return high, low


def kernel(
    narrow, wide, cut, in_hbm, out_hbm, x_hbm, o_ref,
    in_ref, out_pat_ref, blocks, row_parts, left, total, sums, load_sem, send_sem, recv_sem,
    row_send, row_recv, sum_send, sum_recv,
):
    rows, cols = x_hbm.shape
    blks = in_ref.shape[0]
    units = cols // LANES
    line = wide // 4
    group = wide // narrow
    n = lax.axis_index("narrow")
    w = lax.axis_index("wide")
    z, y, c = w // 4, (w // 2) % 2, w % 2

    def index(zz, yy, cc):
        return (zz * 2 + yy) * 2 + cc

    def partner(kind):
        return {
            UP: (n, index(z + 1, y, c)),
            DOWN: (n, index(z - 1, y, c)),
            ACROSS: (n, index(z, 1 - y, c)),
            SIBLING: (n, index(z, y, 1 - c)),
        }[kind]

    loads = [
        pltpu.make_async_copy(source, target, load_sem.at[i])
        for i, (source, target) in enumerate(
            [
                (x_hbm, blocks.at[c, z, y]),
                (x_hbm, row_parts.at[n]),
                (in_hbm, in_ref),
                (out_hbm, out_pat_ref),
            ]
        )
    ]
    for load in loads:
        load.start()

    has_up, has_down = z + 1 < line, z >= 1
    others = [lax.rem(n + d, narrow) for d in range(1, narrow)]

    barrier = pltpu.get_barrier_semaphore()

    def greet(device):
        pl.semaphore_signal(barrier, inc=1, device_id=device, device_id_type=MESH)

    greet(partner(ACROSS))
    greet(partner(SIBLING))
    for other in others:
        greet((other, w))

    @pl.when(has_up)
    def _():
        greet(partner(UP))

    @pl.when(has_down)
    def _():
        greet(partner(DOWN))

    def keep(pattern, shard, part, u):
        first = (shard * rows) // BLK
        second = jnp.minimum(first + 1, blks - 1)
        col = (part * cols + u * LANES) // BLK
        upper = lax.broadcasted_iota(jnp.int32, (rows, LANES), 0) < (first + 1) * BLK - shard * rows
        return jnp.where(
            upper, pattern[first, col].astype(jnp.float32), pattern[second, col].astype(jnp.float32)
        )

    def keep_all(shard, part):
        return jnp.concatenate([keep(in_ref, shard, part, u) for u in range(units)], axis=1)

    met = 1 + 1 + len(others) + has_up.astype(jnp.int32) + has_down.astype(jnp.int32)
    pl.semaphore_wait(barrier, met)

    low, rest = pl.ds(0, 2 * cut), pl.ds(2 * cut, rows - 2 * cut)

    def piece(core, plane, yy, part):
        return blocks.at[core, plane, yy, pl.ds(part * cut, cut), :]

    def both_rest(core, plane):
        return blocks.at[core, plane, :, rest, :]

    def copy(kind, ref, plane, number, source=None):
        via = {UP: 0, DOWN: 0, ACROSS: 1, SIBLING: 2}[kind]
        return pltpu.make_async_remote_copy(
            src_ref=ref if source is None else source,
            dst_ref=ref,
            send_sem=send_sem.at[kind, plane, number],
            recv_sem=recv_sem.at[via, plane, number],
            device_id=partner(kind),
            device_id_type=MESH,
        )

    def start(kind, ref, plane, number, source=None):
        one = copy(kind, ref, plane, number, source)
        if kind == UP:
            pl.when(has_up)(one.start)
        elif kind == DOWN:
            pl.when(has_down)(one.start)
        else:
            one.start()

    def finish(kind, ref, plane, number, source=None):
        one = copy(kind, ref, plane, number, source)
        if kind == UP:
            pl.when(has_up)(one.wait_send)
        elif kind == DOWN:
            pl.when(has_down)(one.wait_send)
        else:
            one.wait_send()

    def arrive(kind, ref, plane, number):
        copy(kind, ref, plane, number).wait_recv()

    def nothing(*_):
        pass

    def row_copy(other):
        return pltpu.make_async_remote_copy(
            src_ref=x_hbm,
            dst_ref=row_parts.at[n],
            send_sem=row_send.at[other],
            recv_sem=row_recv.at[n],
            device_id=(other, w),
            device_id_type=MESH,
        )

    def row_arrival(other):
        return pltpu.make_async_remote_copy(
            src_ref=x_hbm,
            dst_ref=row_parts.at[other],
            send_sem=row_send.at[other],
            recv_sem=row_recv.at[other],
            device_id=(other, w),
            device_id_type=MESH,
        )

    def own(act):
        act(ACROSS, blocks.at[c, z, y, rest, :], z, 2, x_hbm.at[rest, :])
        for part in range(2):
            ref = piece(c, z, y, part)
            for kind in (UP, DOWN, ACROSS):
                act(kind, ref, z, part, x_hbm.at[pl.ds(part * cut, cut), :])
        act(SIBLING, blocks.at[c, z, y, low, :], z, 0, x_hbm.at[low, :])

    def beside(wait, act):
        wait(ACROSS, blocks.at[c, z, 1 - y, rest, :], z, 2)
        for kind in (UP, DOWN, SIBLING):
            act(kind, both_rest(c, z), z, 2)

    def from_across(plane, wait, act):
        for part in range(2):
            wait(ACROSS, piece(c, plane, 1 - y, part), plane, part)
        act(SIBLING, blocks.at[c, plane, 1 - y, low, :], plane, 1)

    def sides(step, visit):
        pl.when(z >= step)(lambda: visit(z - step, UP))
        pl.when(z + step < line)(lambda: visit(z + step, DOWN))

    def along_line(step, wait, act):
        for part in range(2):

            def one_piece(plane, kind):
                ref = piece(c, plane, y, part)
                wait(LINE, ref, plane, part)
                act(kind, ref, plane, part)
                act(ACROSS, ref, plane, part)
                if part == 1:
                    act(SIBLING, blocks.at[c, plane, y, low, :], plane, 0)

            sides(step, one_piece)

    def rest_of_line(step, wait, act):
        def the_rest(plane, kind):
            ref = both_rest(c, plane)
            wait(LINE, ref, plane, 2)
            act(kind, ref, plane, 2)
            act(SIBLING, ref, plane, 2)

        sides(step, the_rest)

    def half(plane, core):
        masked = [blocks[core, plane, yy] * keep_all(index(plane, yy, core), n) for yy in range(2)]
        b_high, b_low = split(jnp.concatenate(masked, axis=0))
        pair = left[plane, core]
        first_two = jnp.dot(pair, b_high, preferred_element_type=jnp.float32)
        term = first_two[:rows] + first_two[rows:]
        total[...] += term + jnp.dot(pair[:rows], b_low, preferred_element_type=jnp.float32)

    def multiply(plane):
        def one_half(h, carry):
            @pl.when(h == 1)
            def _():
                arrive(SIBLING, blocks.at[1 - c, plane, y, low, :], plane, 0)
                arrive(SIBLING, blocks.at[1 - c, plane, 1 - y, low, :], plane, 1)
                arrive(SIBLING, both_rest(1 - c, plane), plane, 2)

            half(plane, (c + h) % 2)
            return carry

        lax.fori_loop(0, 2, one_half, 0)

    own(start)
    for other in others:
        row_copy(other).start()
    total[...] = jnp.zeros_like(total)
    for load in loads:
        load.wait()
    beside(arrive, start)

    def prepare():
        for other in others:
            row_arrival(other).wait_recv()
        for g in range(narrow):
            both = jnp.concatenate(split(row_parts[g] * keep_all(w, g)), axis=0)
            for q in range(group // 4):
                for core in range(2):
                    begins = [(q * 4 + 2 * yy + core) * rows for yy in range(2)]
                    left[g * (group // 4) + q, core] = jnp.concatenate(
                        [both[:, begin : begin + rows] for begin in begins], axis=1
                    )

    def late(step):
        @pl.when(step == 0)
        def _():
            from_across(z, arrive, start)
            prepare()

        @pl.when(step > 0)
        def _():
            sides(step, lambda plane, kind: from_across(plane, arrive, start))

        def one_side(side, carry):
            plane = z + (2 * side - 1) * step
            live = (plane >= 0) & (plane < line) & ((step > 0) | (side == 0))
            pl.when(live)(lambda: multiply(plane))
            return carry

        lax.fori_loop(0, 2, one_side, 0)

    at_end = (z == 0) | (z == line - 1)

    def turn(step, carry):
        along_line(step, arrive, start)
        pl.when(at_end)(lambda: late(step - 1))
        rest_of_line(step, arrive, start)
        pl.when(jnp.logical_not(at_end))(lambda: late(step - 1))
        return carry

    lax.fori_loop(1, line + 1, turn, 0)

    expanded = total[...]
    partial = None
    for u in range(units):
        at = slice(u * LANES, (u + 1) * LANES)
        inflated = expanded[:, at] * expanded[:, at] * keep(out_pat_ref, w, n, u)
        o_ref[:, at] = inflated
        partial = inflated if partial is None else partial + inflated
    sums[n] = partial

    def sum_copy(other, slot):
        return pltpu.make_async_remote_copy(
            src_ref=sums.at[n],
            dst_ref=sums.at[slot],
            send_sem=sum_send.at[other],
            recv_sem=sum_recv.at[slot],
            device_id=(other, w),
            device_id_type=MESH,
        )

    for other in others:
        sum_copy(other, n).start()

    own(finish)
    beside(nothing, finish)
    from_across(z, nothing, finish)

    def drain_turn(step, carry):
        along_line(step, nothing, finish)
        rest_of_line(step, nothing, finish)
        sides(step, lambda plane, kind: from_across(plane, nothing, finish))
        return carry

    lax.fori_loop(1, line, drain_turn, 0)
    for other in others:
        row_copy(other).wait_send()
    for other in others:
        sum_copy(other, other).wait_recv()
    row_sum = sums[0]
    for g in range(1, narrow):
        row_sum = row_sum + sums[g]
    scale = (cols * narrow) / jnp.sum(row_sum, axis=1, keepdims=True)
    o_ref[...] = o_ref[...] * scale
    for other in others:
        sum_copy(other, n).wait_send()


def body(narrow, wide, state, in_pattern, out_pattern):
    rows, cols = state.shape
    cut = 2 * rows // 5
    line = wide // 4
    hbm = pl.BlockSpec(memory_space=pltpu.HBM)
    vmem = pl.BlockSpec(memory_space=pltpu.VMEM)
    flops = 2 * rows * cols * cols * narrow
    return pl.pallas_call(
        functools.partial(kernel, narrow, wide, cut),
        out_shape=pltpu.VMEM((rows, cols), jnp.float32),
        in_specs=[hbm, hbm, hbm],
        out_specs=vmem,
        scratch_shapes=[
            pltpu.SMEM(in_pattern.shape, jnp.int32),
            pltpu.SMEM(out_pattern.shape, jnp.int32),
            pltpu.VMEM((2, line, 2, rows, cols), jnp.float32),
            pltpu.VMEM((narrow, rows, cols), jnp.float32),
            pltpu.VMEM((line, 2, 2 * rows, 2 * rows), jnp.bfloat16),
            pltpu.VMEM((rows, cols), jnp.float32),
            pltpu.VMEM((narrow, rows, LANES), jnp.float32),
            pltpu.SemaphoreType.DMA((4,)),
            pltpu.SemaphoreType.DMA((4, line, 3)),
            pltpu.SemaphoreType.DMA((3, line, 3)),
            pltpu.SemaphoreType.DMA((narrow,)),
            pltpu.SemaphoreType.DMA((narrow,)),
            pltpu.SemaphoreType.DMA((narrow,)),
            pltpu.SemaphoreType.DMA((narrow,)),
        ],
        compiler_params=pltpu.CompilerParams(
            collective_id=0, has_side_effects=True, vmem_limit_bytes=48 * 1024 * 1024
        ),
        cost_estimate=pl.CostEstimate(flops=flops, bytes_accessed=8 * rows * cols, transcendentals=0),
    )(*[pltpu.with_memory_space_constraint(a, pltpu.HBM) for a in (in_pattern, out_pattern, state)])


def solution(mesh):
    return jax.shard_map(
        functools.partial(body, mesh.shape["narrow"], mesh.shape["wide"]),
        mesh=mesh,
        in_specs=(P("wide", "narrow"), P(), P()),
        out_specs=P("wide", "narrow"),
        check_vma=False,
    )
```

```python
import functools

import jax
import jax.numpy as jnp
from jax import lax
from jax.experimental import pallas as pl
from jax.experimental.pallas import tpu as pltpu
from jax.sharding import PartitionSpec as P

BLK = 256
LANES = 128
MESH = pl.DeviceIdType.MESH
UP, DOWN, ACROSS, SIBLING = range(4)
LINE = UP


def split(value):
    high = value.astype(jnp.bfloat16)
    low = (value - high.astype(jnp.float32)).astype(jnp.bfloat16)
    return high, low


def kernel(
    narrow, wide, cut, in_hbm, out_hbm, x_hbm, o_ref,
    in_ref, out_pat_ref, blocks, row_parts, left, total, sums, load_sem, send_sem, recv_sem,
    row_send, row_recv, sum_send, sum_recv,
):
    rows, cols = x_hbm.shape
    blks = in_ref.shape[0]
    units = cols // LANES
    line = wide // 4
    group = wide // narrow
    n = lax.axis_index("narrow")
    w = lax.axis_index("wide")
    z, y, c = w // 4, (w // 2) % 2, w % 2

    def index(zz, yy, cc):
        return (zz * 2 + yy) * 2 + cc

    def partner(kind):
        return {
            UP: (n, index(z + 1, y, c)),
            DOWN: (n, index(z - 1, y, c)),
            ACROSS: (n, index(z, 1 - y, c)),
            SIBLING: (n, index(z, y, 1 - c)),
        }[kind]

    loads = [
        pltpu.make_async_copy(source, target, load_sem.at[i])
        for i, (source, target) in enumerate(
            [(x_hbm, blocks.at[c, z, y]), (in_hbm, in_ref), (out_hbm, out_pat_ref)]
        )
    ]
    for load in loads:
        load.start()

    has_up, has_down = z + 1 < line, z >= 1
    others = [lax.rem(n + d, narrow) for d in range(1, narrow)]

    barrier = pltpu.get_barrier_semaphore()

    def greet(device):
        pl.semaphore_signal(barrier, inc=1, device_id=device, device_id_type=MESH)

    greet(partner(ACROSS))
    greet(partner(SIBLING))
    for other in others:
        greet((other, w))

    @pl.when(has_up)
    def _():
        greet(partner(UP))

    @pl.when(has_down)
    def _():
        greet(partner(DOWN))

    first = (w * rows) // BLK
    second = jnp.minimum(first + 1, blks - 1)
    upper = lax.broadcasted_iota(jnp.int32, (rows, LANES), 0) < (first + 1) * BLK - w * rows

    def keep(pattern, u):
        col = (n * cols + u * LANES) // BLK
        return jnp.where(
            upper, pattern[first, col].astype(jnp.float32), pattern[second, col].astype(jnp.float32)
        )

    for load in loads:
        load.wait()
    for u in range(units):
        at = slice(u * LANES, (u + 1) * LANES)
        masked = blocks[c, z, y, :, at] * keep(in_ref, u)
        blocks[c, z, y, :, at] = masked
        row_parts[n, :, at] = masked

    met = 1 + 1 + len(others) + has_up.astype(jnp.int32) + has_down.astype(jnp.int32)
    pl.semaphore_wait(barrier, met)

    low, rest = pl.ds(0, cut[1]), pl.ds(cut[1], rows - cut[1])

    def piece(core, plane, yy, part):
        return blocks.at[core, plane, yy, pl.ds((0, cut[0])[part], (cut[0], cut[1] - cut[0])[part]), :]

    def both_rest(core, plane):
        return blocks.at[core, plane, :, rest, :]

    def copy(kind, ref, plane, number):
        via = {UP: 0, DOWN: 0, ACROSS: 1, SIBLING: 2}[kind]
        return pltpu.make_async_remote_copy(
            src_ref=ref,
            dst_ref=ref,
            send_sem=send_sem.at[kind, plane, number],
            recv_sem=recv_sem.at[via, plane, number],
            device_id=partner(kind),
            device_id_type=MESH,
        )

    def start(kind, ref, plane, number):
        one = copy(kind, ref, plane, number)
        if kind == UP:
            pl.when(has_up)(one.start)
        elif kind == DOWN:
            pl.when(has_down)(one.start)
        else:
            one.start()

    def finish(kind, ref, plane, number):
        one = copy(kind, ref, plane, number)
        if kind == UP:
            pl.when(has_up)(one.wait_send)
        elif kind == DOWN:
            pl.when(has_down)(one.wait_send)
        else:
            one.wait_send()

    def arrive(kind, ref, plane, number):
        copy(kind, ref, plane, number).wait_recv()

    def nothing(*_):
        pass

    def row_copy(other):
        return pltpu.make_async_remote_copy(
            src_ref=blocks.at[c, z, y],
            dst_ref=row_parts.at[n],
            send_sem=row_send.at[other],
            recv_sem=row_recv.at[n],
            device_id=(other, w),
            device_id_type=MESH,
        )

    def row_arrival(other):
        return pltpu.make_async_remote_copy(
            src_ref=blocks.at[c, z, y],
            dst_ref=row_parts.at[other],
            send_sem=row_send.at[other],
            recv_sem=row_recv.at[other],
            device_id=(other, w),
            device_id_type=MESH,
        )

    def own(act):
        act(ACROSS, blocks.at[c, z, y, rest, :], z, 2)
        for part in range(2):
            ref = piece(c, z, y, part)
            for kind in (UP, DOWN, ACROSS):
                act(kind, ref, z, part)
        act(SIBLING, blocks.at[c, z, y, low, :], z, 0)

    def beside(wait, act):
        wait(ACROSS, blocks.at[c, z, 1 - y, rest, :], z, 2)
        for kind in (UP, DOWN, SIBLING):
            act(kind, both_rest(c, z), z, 2)

    def from_across(plane, wait, act):
        for part in range(2):
            wait(ACROSS, piece(c, plane, 1 - y, part), plane, part)
        act(SIBLING, blocks.at[c, plane, 1 - y, low, :], plane, 1)

    def sides(step, visit):
        pl.when(z >= step)(lambda: visit(z - step, UP))
        pl.when(z + step < line)(lambda: visit(z + step, DOWN))

    def along_line(step, wait, act):
        for part in range(2):

            def one_piece(plane, kind):
                ref = piece(c, plane, y, part)
                wait(LINE, ref, plane, part)
                act(kind, ref, plane, part)
                act(ACROSS, ref, plane, part)
                if part == 1:
                    act(SIBLING, blocks.at[c, plane, y, low, :], plane, 0)

            sides(step, one_piece)

    def rest_of_line(step, wait, act):
        def the_rest(plane, kind):
            ref = both_rest(c, plane)
            wait(LINE, ref, plane, 2)
            act(kind, ref, plane, 2)
            act(SIBLING, ref, plane, 2)

        sides(step, the_rest)

    def half(plane, core):
        b_high, b_low = split(blocks[core, plane].reshape(2 * rows, cols))
        pair = left[plane, core]
        first_two = jnp.dot(pair, b_high, preferred_element_type=jnp.float32)
        term = first_two[:rows] + first_two[rows:]
        total[...] += term + jnp.dot(pair[:rows], b_low, preferred_element_type=jnp.float32)

    def multiply(plane):
        def one_half(h, carry):
            @pl.when(h == 1)
            def _():
                arrive(SIBLING, blocks.at[1 - c, plane, y, low, :], plane, 0)
                arrive(SIBLING, blocks.at[1 - c, plane, 1 - y, low, :], plane, 1)
                arrive(SIBLING, both_rest(1 - c, plane), plane, 2)

            half(plane, (c + h) % 2)
            return carry

        lax.fori_loop(0, 2, one_half, 0)

    own(start)
    for other in others:
        row_copy(other).start()
    total[...] = jnp.zeros_like(total)
    beside(arrive, start)

    def prepare():
        for other in others:
            row_arrival(other).wait_recv()
        for g in range(narrow):
            both = jnp.concatenate(split(row_parts[g]), axis=0)
            for q in range(group // 4):
                for core in range(2):
                    begins = [(q * 4 + 2 * yy + core) * rows for yy in range(2)]
                    left[g * (group // 4) + q, core] = jnp.concatenate(
                        [both[:, begin : begin + rows] for begin in begins], axis=1
                    )

    def late(step):
        @pl.when(step == 0)
        def _():
            from_across(z, arrive, start)
            prepare()

        @pl.when(step > 0)
        def _():
            sides(step, lambda plane, kind: from_across(plane, arrive, start))

        def one_side(side, carry):
            plane = z + (2 * side - 1) * step
            live = (plane >= 0) & (plane < line) & ((step > 0) | (side == 0))
            pl.when(live)(lambda: multiply(plane))
            return carry

        lax.fori_loop(0, 2, one_side, 0)

    at_end = (z == 0) | (z == line - 1)

    def turn(step, carry):
        along_line(step, arrive, start)
        pl.when(at_end)(lambda: late(step - 1))
        rest_of_line(step, arrive, start)
        pl.when(jnp.logical_not(at_end))(lambda: late(step - 1))
        return carry

    lax.fori_loop(1, line + 1, turn, 0)

    expanded = total[...]
    partial = None
    for u in range(units):
        at = slice(u * LANES, (u + 1) * LANES)
        inflated = expanded[:, at] * expanded[:, at] * keep(out_pat_ref, u)
        o_ref[:, at] = inflated
        partial = inflated if partial is None else partial + inflated
    sums[n] = partial

    def sum_copy(other, slot):
        return pltpu.make_async_remote_copy(
            src_ref=sums.at[n],
            dst_ref=sums.at[slot],
            send_sem=sum_send.at[other],
            recv_sem=sum_recv.at[slot],
            device_id=(other, w),
            device_id_type=MESH,
        )

    for other in others:
        sum_copy(other, n).start()

    own(finish)
    beside(nothing, finish)
    from_across(z, nothing, finish)

    def drain_turn(step, carry):
        along_line(step, nothing, finish)
        rest_of_line(step, nothing, finish)
        sides(step, lambda plane, kind: from_across(plane, nothing, finish))
        return carry

    lax.fori_loop(1, line, drain_turn, 0)
    for other in others:
        row_copy(other).wait_send()
    for other in others:
        sum_copy(other, other).wait_recv()
    row_sum = sums[0]
    for g in range(1, narrow):
        row_sum = row_sum + sums[g]
    scale = (cols * narrow) / jnp.sum(row_sum, axis=1, keepdims=True)
    o_ref[...] = o_ref[...] * scale
    for other in others:
        sum_copy(other, n).wait_send()


def body(narrow, wide, state, in_pattern, out_pattern):
    rows, cols = state.shape
    cut = (rows // 2, 9 * rows // 10)
    line = wide // 4
    hbm = pl.BlockSpec(memory_space=pltpu.HBM)
    vmem = pl.BlockSpec(memory_space=pltpu.VMEM)
    flops = 2 * rows * cols * cols * narrow
    return pl.pallas_call(
        functools.partial(kernel, narrow, wide, cut),
        out_shape=pltpu.VMEM((rows, cols), jnp.float32),
        in_specs=[hbm, hbm, hbm],
        out_specs=vmem,
        scratch_shapes=[
            pltpu.SMEM(in_pattern.shape, jnp.int32),
            pltpu.SMEM(out_pattern.shape, jnp.int32),
            pltpu.VMEM((2, line, 2, rows, cols), jnp.float32),
            pltpu.VMEM((narrow, rows, cols), jnp.float32),
            pltpu.VMEM((line, 2, 2 * rows, 2 * rows), jnp.bfloat16),
            pltpu.VMEM((rows, cols), jnp.float32),
            pltpu.VMEM((narrow, rows, LANES), jnp.float32),
            pltpu.SemaphoreType.DMA((3,)),
            pltpu.SemaphoreType.DMA((4, line, 3)),
            pltpu.SemaphoreType.DMA((3, line, 3)),
            pltpu.SemaphoreType.DMA((narrow,)),
            pltpu.SemaphoreType.DMA((narrow,)),
            pltpu.SemaphoreType.DMA((narrow,)),
            pltpu.SemaphoreType.DMA((narrow,)),
        ],
        compiler_params=pltpu.CompilerParams(
            collective_id=0, has_side_effects=True, vmem_limit_bytes=48 * 1024 * 1024
        ),
        cost_estimate=pl.CostEstimate(flops=flops, bytes_accessed=8 * rows * cols, transcendentals=0),
    )(*[pltpu.with_memory_space_constraint(a, pltpu.HBM) for a in (in_pattern, out_pattern, state)])


def solution(mesh):
    return jax.shard_map(
        functools.partial(body, mesh.shape["narrow"], mesh.shape["wide"]),
        mesh=mesh,
        in_specs=(P("wide", "narrow"), P(), P()),
        out_specs=P("wide", "narrow"),
        check_vma=False,
    )
```

```python
import functools

import jax
import jax.numpy as jnp
from jax import lax
from jax.experimental import pallas as pl
from jax.experimental.pallas import tpu as pltpu
from jax.sharding import PartitionSpec as P

BLK = 256
LANES = 128
MESH = pl.DeviceIdType.MESH
UP, DOWN, ACROSS, SIBLING = range(4)
LINE = UP


def split(value):
    high = value.astype(jnp.bfloat16)
    low = (value - high.astype(jnp.float32)).astype(jnp.bfloat16)
    return high, low


def kernel(
    narrow, wide, cut, in_hbm, out_hbm, x_hbm, o_ref,
    in_ref, out_pat_ref, blocks, row_parts, left, total, sums, load_sem, send_sem, recv_sem,
    row_send, row_recv, sum_send, sum_recv,
):
    rows, cols = x_hbm.shape
    blks = in_ref.shape[0]
    units = cols // LANES
    line = wide // 4
    group = wide // narrow
    n = lax.axis_index("narrow")
    w = lax.axis_index("wide")
    z, y, c = w // 4, (w // 2) % 2, w % 2

    def index(zz, yy, cc):
        return (zz * 2 + yy) * 2 + cc

    def partner(kind):
        return {
            UP: (n, index(z + 1, y, c)),
            DOWN: (n, index(z - 1, y, c)),
            ACROSS: (n, index(z, 1 - y, c)),
            SIBLING: (n, index(z, y, 1 - c)),
        }[kind]

    loads = [
        pltpu.make_async_copy(source, target, load_sem.at[i])
        for i, (source, target) in enumerate(
            [(x_hbm, blocks.at[c, z, y]), (in_hbm, in_ref), (out_hbm, out_pat_ref)]
        )
    ]
    for load in loads:
        load.start()

    has_up, has_down = z + 1 < line, z >= 1
    others = [lax.rem(n + d, narrow) for d in range(1, narrow)]

    barrier = pltpu.get_barrier_semaphore()

    def greet(device):
        pl.semaphore_signal(barrier, inc=1, device_id=device, device_id_type=MESH)

    greet(partner(ACROSS))
    greet(partner(SIBLING))
    for other in others:
        greet((other, w))

    @pl.when(has_up)
    def _():
        greet(partner(UP))

    @pl.when(has_down)
    def _():
        greet(partner(DOWN))

    first = (w * rows) // BLK
    second = jnp.minimum(first + 1, blks - 1)
    upper = lax.broadcasted_iota(jnp.int32, (rows, LANES), 0) < (first + 1) * BLK - w * rows

    def keep(pattern, u):
        col = (n * cols + u * LANES) // BLK
        return jnp.where(
            upper, pattern[first, col].astype(jnp.float32), pattern[second, col].astype(jnp.float32)
        )

    for load in loads:
        load.wait()
    for u in range(units):
        at = slice(u * LANES, (u + 1) * LANES)
        masked = blocks[c, z, y, :, at] * keep(in_ref, u)
        blocks[c, z, y, :, at] = masked
        row_parts[n, :, at] = masked

    met = 1 + 1 + len(others) + has_up.astype(jnp.int32) + has_down.astype(jnp.int32)
    pl.semaphore_wait(barrier, met)

    low, rest = pl.ds(0, 2 * cut), pl.ds(2 * cut, rows - 2 * cut)

    def piece(core, plane, yy, part):
        return blocks.at[core, plane, yy, pl.ds(part * cut, cut), :]

    def both_rest(core, plane):
        return blocks.at[core, plane, :, rest, :]

    def copy(kind, ref, plane, number):
        via = {UP: 0, DOWN: 0, ACROSS: 1, SIBLING: 2}[kind]
        return pltpu.make_async_remote_copy(
            src_ref=ref,
            dst_ref=ref,
            send_sem=send_sem.at[kind, plane, number],
            recv_sem=recv_sem.at[via, plane, number],
            device_id=partner(kind),
            device_id_type=MESH,
        )

    def start(kind, ref, plane, number):
        one = copy(kind, ref, plane, number)
        if kind == UP:
            pl.when(has_up)(one.start)
        elif kind == DOWN:
            pl.when(has_down)(one.start)
        else:
            one.start()

    def finish(kind, ref, plane, number):
        one = copy(kind, ref, plane, number)
        if kind == UP:
            pl.when(has_up)(one.wait_send)
        elif kind == DOWN:
            pl.when(has_down)(one.wait_send)
        else:
            one.wait_send()

    def arrive(kind, ref, plane, number):
        copy(kind, ref, plane, number).wait_recv()

    def nothing(*_):
        pass

    def row_copy(other):
        return pltpu.make_async_remote_copy(
            src_ref=blocks.at[c, z, y],
            dst_ref=row_parts.at[n],
            send_sem=row_send.at[other],
            recv_sem=row_recv.at[n],
            device_id=(other, w),
            device_id_type=MESH,
        )

    def row_arrival(other):
        return pltpu.make_async_remote_copy(
            src_ref=blocks.at[c, z, y],
            dst_ref=row_parts.at[other],
            send_sem=row_send.at[other],
            recv_sem=row_recv.at[other],
            device_id=(other, w),
            device_id_type=MESH,
        )

    def own(act):
        act(ACROSS, blocks.at[c, z, y, rest, :], z, 2)
        for part in range(2):
            ref = piece(c, z, y, part)
            for kind in (UP, DOWN, ACROSS):
                act(kind, ref, z, part)
        act(SIBLING, blocks.at[c, z, y, low, :], z, 0)

    def beside(wait, act):
        wait(ACROSS, blocks.at[c, z, 1 - y, rest, :], z, 2)
        for kind in (UP, DOWN, SIBLING):
            act(kind, both_rest(c, z), z, 2)

    def from_across(plane, wait, act):
        for part in range(2):
            wait(ACROSS, piece(c, plane, 1 - y, part), plane, part)
        act(SIBLING, blocks.at[c, plane, 1 - y, low, :], plane, 1)

    def sides(step, visit):
        pl.when(z >= step)(lambda: visit(z - step, UP))
        pl.when(z + step < line)(lambda: visit(z + step, DOWN))

    def along_line(step, wait, act):
        for part in range(2):

            def one_piece(plane, kind):
                ref = piece(c, plane, y, part)
                wait(LINE, ref, plane, part)
                act(kind, ref, plane, part)
                act(ACROSS, ref, plane, part)
                if part == 1:
                    act(SIBLING, blocks.at[c, plane, y, low, :], plane, 0)

            sides(step, one_piece)

    def rest_of_line(step, wait, act):
        def the_rest(plane, kind):
            ref = both_rest(c, plane)
            wait(LINE, ref, plane, 2)
            act(kind, ref, plane, 2)
            act(SIBLING, ref, plane, 2)

        sides(step, the_rest)

    def half(plane, core):
        b_high, b_low = split(blocks[core, plane].reshape(2 * rows, cols))
        pair = left[plane, core]
        first_two = jnp.dot(pair, b_high, preferred_element_type=jnp.float32)
        term = first_two[:rows] + first_two[rows:]
        total[...] += term + jnp.dot(pair[:rows], b_low, preferred_element_type=jnp.float32)

    def multiply(plane):
        def one_half(h, carry):
            @pl.when(h == 1)
            def _():
                arrive(SIBLING, blocks.at[1 - c, plane, y, low, :], plane, 0)
                arrive(SIBLING, blocks.at[1 - c, plane, 1 - y, low, :], plane, 1)
                arrive(SIBLING, both_rest(1 - c, plane), plane, 2)

            half(plane, (c + h) % 2)
            return carry

        lax.fori_loop(0, 2, one_half, 0)

    own(start)
    for other in others:
        row_copy(other).start()
    total[...] = jnp.zeros_like(total)
    beside(arrive, start)

    def prepare():
        for other in others:
            row_arrival(other).wait_recv()
        for g in range(narrow):
            both = jnp.concatenate(split(row_parts[g]), axis=0)
            for q in range(group // 4):
                for core in range(2):
                    begins = [(q * 4 + 2 * yy + core) * rows for yy in range(2)]
                    left[g * (group // 4) + q, core] = jnp.concatenate(
                        [both[:, begin : begin + rows] for begin in begins], axis=1
                    )

    def late(step):
        @pl.when(step == 0)
        def _():
            from_across(z, arrive, start)
            prepare()

        @pl.when(step > 0)
        def _():
            sides(step, lambda plane, kind: from_across(plane, arrive, start))

        def one_side(side, carry):
            plane = z + (2 * side - 1) * step
            live = (plane >= 0) & (plane < line) & ((step > 0) | (side == 0))
            pl.when(live)(lambda: multiply(plane))
            return carry

        lax.fori_loop(0, 2, one_side, 0)

    at_end = (z == 0) | (z == line - 1)

    def drain_line(step, carry):
        along_line(step, nothing, finish)
        rest_of_line(step, nothing, finish)
        return carry

    def turn(step, carry):
        @pl.when(step == line - 1)
        def _():
            own(finish)
            beside(nothing, finish)
            from_across(z, nothing, finish)
            lax.fori_loop(1, line - 2, drain_line, 0)

        along_line(step, arrive, start)
        pl.when(at_end)(lambda: late(step - 1))
        rest_of_line(step, arrive, start)
        pl.when(jnp.logical_not(at_end))(lambda: late(step - 1))
        return carry

    lax.fori_loop(1, line + 1, turn, 0)

    expanded = total[...]
    partial = None
    for u in range(units):
        at = slice(u * LANES, (u + 1) * LANES)
        inflated = expanded[:, at] * expanded[:, at] * keep(out_pat_ref, u)
        o_ref[:, at] = inflated
        partial = inflated if partial is None else partial + inflated
    wide_sums = jnp.broadcast_to(jnp.sum(partial, axis=1, keepdims=True), (rows, LANES))
    padded = jnp.concatenate([wide_sums, jnp.ones((LANES - rows, LANES), jnp.float32)], axis=0)
    sums[n] = padded.T[:8]

    def sum_copy(other, slot):
        return pltpu.make_async_remote_copy(
            src_ref=sums.at[n],
            dst_ref=sums.at[slot],
            send_sem=sum_send.at[other],
            recv_sem=sum_recv.at[slot],
            device_id=(other, w),
            device_id_type=MESH,
        )

    for other in others:
        sum_copy(other, n).start()

    def drain_across(step, carry):
        sides(step, lambda plane, kind: from_across(plane, nothing, finish))
        return carry

    lax.fori_loop(line - 2, line, drain_line, 0)
    lax.fori_loop(1, line, drain_across, 0)
    for other in others:
        row_copy(other).wait_send()
    for other in others:
        sum_copy(other, other).wait_recv()
    row_sum = sums[0]
    for g in range(1, narrow):
        row_sum = row_sum + sums[g]
    spread = jnp.broadcast_to(row_sum[:1], (LANES, LANES)).T[:rows]
    scale = (cols * narrow) / spread
    for u in range(units):
        at = slice(u * LANES, (u + 1) * LANES)
        o_ref[:, at] = o_ref[:, at] * scale
    for other in others:
        sum_copy(other, n).wait_send()


def body(narrow, wide, state, in_pattern, out_pattern):
    rows, cols = state.shape
    cut = 2 * rows // 5
    line = wide // 4
    hbm = pl.BlockSpec(memory_space=pltpu.HBM)
    vmem = pl.BlockSpec(memory_space=pltpu.VMEM)
    flops = 2 * rows * cols * cols * narrow
    return pl.pallas_call(
        functools.partial(kernel, narrow, wide, cut),
        out_shape=pltpu.VMEM((rows, cols), jnp.float32),
        in_specs=[hbm, hbm, hbm],
        out_specs=vmem,
        scratch_shapes=[
            pltpu.SMEM(in_pattern.shape, jnp.int32),
            pltpu.SMEM(out_pattern.shape, jnp.int32),
            pltpu.VMEM((2, line, 2, rows, cols), jnp.float32),
            pltpu.VMEM((narrow, rows, cols), jnp.float32),
            pltpu.VMEM((line, 2, 2 * rows, 2 * rows), jnp.bfloat16),
            pltpu.VMEM((rows, cols), jnp.float32),
            pltpu.VMEM((narrow, 8, LANES), jnp.float32),
            pltpu.SemaphoreType.DMA((3,)),
            pltpu.SemaphoreType.DMA((4, line, 3)),
            pltpu.SemaphoreType.DMA((3, line, 3)),
            pltpu.SemaphoreType.DMA((narrow,)),
            pltpu.SemaphoreType.DMA((narrow,)),
            pltpu.SemaphoreType.DMA((narrow,)),
            pltpu.SemaphoreType.DMA((narrow,)),
        ],
        compiler_params=pltpu.CompilerParams(
            collective_id=0, has_side_effects=True, vmem_limit_bytes=48 * 1024 * 1024
        ),
        cost_estimate=pl.CostEstimate(flops=flops, bytes_accessed=8 * rows * cols, transcendentals=0),
    )(*[pltpu.with_memory_space_constraint(a, pltpu.HBM) for a in (in_pattern, out_pattern, state)])


def solution(mesh):
    return jax.shard_map(
        functools.partial(body, mesh.shape["narrow"], mesh.shape["wide"]),
        mesh=mesh,
        in_specs=(P("wide", "narrow"), P(), P()),
        out_specs=P("wide", "narrow"),
        check_vma=False,
    )
```

```python
import functools

import jax
import jax.numpy as jnp
from jax import lax
from jax.experimental import pallas as pl
from jax.experimental.pallas import tpu as pltpu
from jax.sharding import PartitionSpec as P

BLK = 256
LANES = 128
MESH = pl.DeviceIdType.MESH
UP, DOWN, ACROSS, SIBLING = range(4)
LINE = UP


def split(value):
    high = value.astype(jnp.bfloat16)
    low = (value - high.astype(jnp.float32)).astype(jnp.bfloat16)
    return high, low


def kernel(
    narrow, wide, cut, in_hbm, out_hbm, x_hbm, o_ref,
    in_ref, out_pat_ref, blocks, row_parts, left, total, sums, load_sem, send_sem, recv_sem,
    row_send, row_recv, sum_send, sum_recv,
):
    rows, cols = x_hbm.shape
    blks = in_ref.shape[0]
    units = cols // LANES
    line = wide // 4
    group = wide // narrow
    n = lax.axis_index("narrow")
    w = lax.axis_index("wide")
    z, y, c = w // 4, (w // 2) % 2, w % 2

    def index(zz, yy, cc):
        return (zz * 2 + yy) * 2 + cc

    def partner(kind):
        return {
            UP: (n, index(z + 1, y, c)),
            DOWN: (n, index(z - 1, y, c)),
            ACROSS: (n, index(z, 1 - y, c)),
            SIBLING: (n, index(z, y, 1 - c)),
        }[kind]

    loads = [
        pltpu.make_async_copy(source, target, load_sem.at[i])
        for i, (source, target) in enumerate(
            [(x_hbm, blocks.at[c, z, y]), (in_hbm, in_ref), (out_hbm, out_pat_ref)]
        )
    ]
    for load in loads:
        load.start()

    has_up, has_down = z + 1 < line, z >= 1
    others = [lax.rem(n + d, narrow) for d in range(1, narrow)]

    barrier = pltpu.get_barrier_semaphore()

    def greet(device):
        pl.semaphore_signal(barrier, inc=1, device_id=device, device_id_type=MESH)

    greet(partner(ACROSS))
    greet(partner(SIBLING))
    for other in others:
        greet((other, w))

    @pl.when(has_up)
    def _():
        greet(partner(UP))

    @pl.when(has_down)
    def _():
        greet(partner(DOWN))

    first = (w * rows) // BLK
    second = jnp.minimum(first + 1, blks - 1)
    upper = lax.broadcasted_iota(jnp.int32, (rows, LANES), 0) < (first + 1) * BLK - w * rows

    def keep(pattern, u):
        col = (n * cols + u * LANES) // BLK
        return jnp.where(
            upper, pattern[first, col].astype(jnp.float32), pattern[second, col].astype(jnp.float32)
        )

    for load in loads:
        load.wait()
    for u in range(units):
        at = slice(u * LANES, (u + 1) * LANES)
        masked = blocks[c, z, y, :, at] * keep(in_ref, u)
        blocks[c, z, y, :, at] = masked
        row_parts[n, :, at] = masked

    met = 1 + 1 + len(others) + has_up.astype(jnp.int32) + has_down.astype(jnp.int32)
    pl.semaphore_wait(barrier, met)

    low, rest = pl.ds(0, 2 * cut), pl.ds(2 * cut, rows - 2 * cut)

    def piece(core, plane, yy, part):
        return blocks.at[core, plane, yy, pl.ds(part * cut, cut), :]

    def both_rest(core, plane):
        return blocks.at[core, plane, :, rest, :]

    def copy(kind, ref, plane, number):
        via = {UP: 0, DOWN: 0, ACROSS: 1, SIBLING: 2}[kind]
        return pltpu.make_async_remote_copy(
            src_ref=ref,
            dst_ref=ref,
            send_sem=send_sem.at[kind, plane, number],
            recv_sem=recv_sem.at[via, plane, number],
            device_id=partner(kind),
            device_id_type=MESH,
        )

    def start(kind, ref, plane, number):
        one = copy(kind, ref, plane, number)
        if kind == UP:
            pl.when(has_up)(one.start)
        elif kind == DOWN:
            pl.when(has_down)(one.start)
        else:
            one.start()

    def finish(kind, ref, plane, number):
        one = copy(kind, ref, plane, number)
        if kind == UP:
            pl.when(has_up)(one.wait_send)
        elif kind == DOWN:
            pl.when(has_down)(one.wait_send)
        else:
            one.wait_send()

    def arrive(kind, ref, plane, number):
        copy(kind, ref, plane, number).wait_recv()

    def nothing(*_):
        pass

    def row_copy(other):
        return pltpu.make_async_remote_copy(
            src_ref=blocks.at[c, z, y],
            dst_ref=row_parts.at[n],
            send_sem=row_send.at[other],
            recv_sem=row_recv.at[n],
            device_id=(other, w),
            device_id_type=MESH,
        )

    def row_arrival(other):
        return pltpu.make_async_remote_copy(
            src_ref=blocks.at[c, z, y],
            dst_ref=row_parts.at[other],
            send_sem=row_send.at[other],
            recv_sem=row_recv.at[other],
            device_id=(other, w),
            device_id_type=MESH,
        )

    def own(act):
        act(ACROSS, blocks.at[c, z, y, rest, :], z, 2)
        for part in range(2):
            ref = piece(c, z, y, part)
            for kind in (UP, DOWN, ACROSS):
                act(kind, ref, z, part)
        act(SIBLING, blocks.at[c, z, y, low, :], z, 0)

    def beside(wait, act):
        wait(ACROSS, blocks.at[c, z, 1 - y, rest, :], z, 2)
        for kind in (UP, DOWN, SIBLING):
            act(kind, both_rest(c, z), z, 2)

    def from_across(plane, wait, act):
        for part in range(2):
            wait(ACROSS, piece(c, plane, 1 - y, part), plane, part)
        act(SIBLING, blocks.at[c, plane, 1 - y, low, :], plane, 1)

    def sides(step, visit):
        pl.when(z >= step)(lambda: visit(z - step, UP))
        pl.when(z + step < line)(lambda: visit(z + step, DOWN))

    def along_line(step, wait, act, between=None):
        for part in range(2):
            if part == 1 and between is not None:
                between()

            def one_piece(plane, kind):
                ref = piece(c, plane, y, part)
                wait(LINE, ref, plane, part)
                act(kind, ref, plane, part)
                act(ACROSS, ref, plane, part)
                if part == 1:
                    act(SIBLING, blocks.at[c, plane, y, low, :], plane, 0)

            sides(step, one_piece)

    def rest_of_line(step, wait, act):
        def the_rest(plane, kind):
            ref = both_rest(c, plane)
            wait(LINE, ref, plane, 2)
            act(kind, ref, plane, 2)
            act(SIBLING, ref, plane, 2)

        sides(step, the_rest)

    def half(plane, core):
        b_high, b_low = split(blocks[core, plane].reshape(2 * rows, cols))
        pair = left[plane, core]
        first_two = jnp.dot(pair, b_high, preferred_element_type=jnp.float32)
        term = first_two[:rows] + first_two[rows:]
        total[...] += term + jnp.dot(pair[:rows], b_low, preferred_element_type=jnp.float32)

    def multiply(plane):
        def one_half(h, carry):
            @pl.when(h == 1)
            def _():
                arrive(SIBLING, blocks.at[1 - c, plane, y, low, :], plane, 0)
                arrive(SIBLING, blocks.at[1 - c, plane, 1 - y, low, :], plane, 1)
                arrive(SIBLING, both_rest(1 - c, plane), plane, 2)

            half(plane, (c + h) % 2)
            return carry

        lax.fori_loop(0, 2, one_half, 0)

    own(start)
    for other in others:
        row_copy(other).start()
    total[...] = jnp.zeros_like(total)
    beside(arrive, start)

    def prepare():
        for other in others:
            row_arrival(other).wait_recv()
        for g in range(narrow):
            both = jnp.concatenate(split(row_parts[g]), axis=0)
            for q in range(group // 4):
                for core in range(2):
                    begins = [(q * 4 + 2 * yy + core) * rows for yy in range(2)]
                    left[g * (group // 4) + q, core] = jnp.concatenate(
                        [both[:, begin : begin + rows] for begin in begins], axis=1
                    )

    def take_across(step):
        pl.when(step == 0)(lambda: from_across(z, arrive, start))
        pl.when(step > 0)(
            lambda: sides(step, lambda plane, kind: from_across(plane, arrive, start))
        )

    def late(step):
        @pl.when(step == 0)
        def _():
            prepare()

        def one_side(side, carry):
            plane = z + (2 * side - 1) * step
            live = (plane >= 0) & (plane < line) & ((step > 0) | (side == 0))
            pl.when(live)(lambda: multiply(plane))
            return carry

        lax.fori_loop(0, 2, one_side, 0)

    at_end = (z == 0) | (z == line - 1)

    def drain_line(step, carry):
        along_line(step, nothing, finish)
        rest_of_line(step, nothing, finish)
        return carry

    def turn(step, carry):
        @pl.when(step == line - 1)
        def _():
            own(finish)
            beside(nothing, finish)
            from_across(z, nothing, finish)
            lax.fori_loop(1, line - 2, drain_line, 0)

        early = at_end & (step > 1)
        along_line(
            step, arrive, start, lambda: pl.when(early)(lambda: take_across(step - 1))
        )
        pl.when(jnp.logical_not(early) & at_end)(lambda: take_across(step - 1))
        pl.when(at_end)(lambda: late(step - 1))
        rest_of_line(step, arrive, start)

        @pl.when(jnp.logical_not(at_end))
        def _():
            take_across(step - 1)
            late(step - 1)

        return carry

    lax.fori_loop(1, line + 1, turn, 0)

    expanded = total[...]
    partial = None
    for u in range(units):
        at = slice(u * LANES, (u + 1) * LANES)
        inflated = expanded[:, at] * expanded[:, at] * keep(out_pat_ref, u)
        o_ref[:, at] = inflated
        partial = inflated if partial is None else partial + inflated
    wide_sums = jnp.broadcast_to(jnp.sum(partial, axis=1, keepdims=True), (rows, LANES))
    padded = jnp.concatenate([wide_sums, jnp.ones((LANES - rows, LANES), jnp.float32)], axis=0)
    sums[n] = padded.T[:8]

    def sum_copy(other, slot):
        return pltpu.make_async_remote_copy(
            src_ref=sums.at[n],
            dst_ref=sums.at[slot],
            send_sem=sum_send.at[other],
            recv_sem=sum_recv.at[slot],
            device_id=(other, w),
            device_id_type=MESH,
        )

    for other in others:
        sum_copy(other, n).start()

    def drain_across(step, carry):
        sides(step, lambda plane, kind: from_across(plane, nothing, finish))
        return carry

    lax.fori_loop(line - 2, line, drain_line, 0)
    lax.fori_loop(1, line, drain_across, 0)
    for other in others:
        row_copy(other).wait_send()
    for other in others:
        sum_copy(other, other).wait_recv()
    row_sum = sums[0]
    for g in range(1, narrow):
        row_sum = row_sum + sums[g]
    spread = jnp.broadcast_to(row_sum[:1], (LANES, LANES)).T[:rows]
    scale = (cols * narrow) / spread
    for u in range(units):
        at = slice(u * LANES, (u + 1) * LANES)
        o_ref[:, at] = o_ref[:, at] * scale
    for other in others:
        sum_copy(other, n).wait_send()


def body(narrow, wide, state, in_pattern, out_pattern):
    rows, cols = state.shape
    cut = 2 * rows // 5
    line = wide // 4
    hbm = pl.BlockSpec(memory_space=pltpu.HBM)
    vmem = pl.BlockSpec(memory_space=pltpu.VMEM)
    flops = 2 * rows * cols * cols * narrow
    return pl.pallas_call(
        functools.partial(kernel, narrow, wide, cut),
        out_shape=pltpu.VMEM((rows, cols), jnp.float32),
        in_specs=[hbm, hbm, hbm],
        out_specs=vmem,
        scratch_shapes=[
            pltpu.SMEM(in_pattern.shape, jnp.int32),
            pltpu.SMEM(out_pattern.shape, jnp.int32),
            pltpu.VMEM((2, line, 2, rows, cols), jnp.float32),
            pltpu.VMEM((narrow, rows, cols), jnp.float32),
            pltpu.VMEM((line, 2, 2 * rows, 2 * rows), jnp.bfloat16),
            pltpu.VMEM((rows, cols), jnp.float32),
            pltpu.VMEM((narrow, 8, LANES), jnp.float32),
            pltpu.SemaphoreType.DMA((3,)),
            pltpu.SemaphoreType.DMA((4, line, 3)),
            pltpu.SemaphoreType.DMA((3, line, 3)),
            pltpu.SemaphoreType.DMA((narrow,)),
            pltpu.SemaphoreType.DMA((narrow,)),
            pltpu.SemaphoreType.DMA((narrow,)),
            pltpu.SemaphoreType.DMA((narrow,)),
        ],
        compiler_params=pltpu.CompilerParams(
            collective_id=0, has_side_effects=True, vmem_limit_bytes=48 * 1024 * 1024
        ),
        cost_estimate=pl.CostEstimate(flops=flops, bytes_accessed=8 * rows * cols, transcendentals=0),
    )(*[pltpu.with_memory_space_constraint(a, pltpu.HBM) for a in (in_pattern, out_pattern, state)])


def solution(mesh):
    return jax.shard_map(
        functools.partial(body, mesh.shape["narrow"], mesh.shape["wide"]),
        mesh=mesh,
        in_specs=(P("wide", "narrow"), P(), P()),
        out_specs=P("wide", "narrow"),
        check_vma=False,
    )
```

```python
import functools

import jax
import jax.numpy as jnp
from jax import lax
from jax.experimental import pallas as pl
from jax.experimental.pallas import tpu as pltpu
from jax.sharding import PartitionSpec as P

BLK = 256
LANES = 128
MESH = pl.DeviceIdType.MESH
UP, DOWN, ACROSS, SIBLING = range(4)
LINE = UP


def split(value):
    high = value.astype(jnp.bfloat16)
    low = (value - high.astype(jnp.float32)).astype(jnp.bfloat16)
    return high, low


def kernel(
    narrow, wide, cut, in_hbm, out_hbm, x_hbm, o_ref,
    in_ref, out_pat_ref, blocks, row_parts, left, total, sums, load_sem, send_sem, recv_sem,
    row_send, row_recv, sum_send, sum_recv,
):
    rows, cols = x_hbm.shape
    blks = in_ref.shape[0]
    units = cols // LANES
    line = wide // 4
    pieces = len(cut) - 1
    group = wide // narrow
    n = lax.axis_index("narrow")
    w = lax.axis_index("wide")
    z, y, c = w // 4, (w // 2) % 2, w % 2

    def index(zz, yy, cc):
        return (zz * 2 + yy) * 2 + cc

    def partner(kind):
        return {
            UP: (n, index(z + 1, y, c)),
            DOWN: (n, index(z - 1, y, c)),
            ACROSS: (n, index(z, 1 - y, c)),
            SIBLING: (n, index(z, y, 1 - c)),
        }[kind]

    loads = [
        pltpu.make_async_copy(source, target, load_sem.at[i])
        for i, (source, target) in enumerate(
            [(x_hbm, blocks.at[c, z, y]), (in_hbm, in_ref), (out_hbm, out_pat_ref)]
        )
    ]
    for load in loads:
        load.start()

    has_up, has_down = z + 1 < line, z >= 1
    others = [lax.rem(n + d, narrow) for d in range(1, narrow)]

    barrier = pltpu.get_barrier_semaphore()

    def greet(device):
        pl.semaphore_signal(barrier, inc=1, device_id=device, device_id_type=MESH)

    greet(partner(ACROSS))
    greet(partner(SIBLING))
    for other in others:
        greet((other, w))

    @pl.when(has_up)
    def _():
        greet(partner(UP))

    @pl.when(has_down)
    def _():
        greet(partner(DOWN))

    first = (w * rows) // BLK
    second = jnp.minimum(first + 1, blks - 1)
    upper = lax.broadcasted_iota(jnp.int32, (rows, LANES), 0) < (first + 1) * BLK - w * rows

    def keep(pattern, u):
        col = (n * cols + u * LANES) // BLK
        return jnp.where(
            upper, pattern[first, col].astype(jnp.float32), pattern[second, col].astype(jnp.float32)
        )

    for load in loads:
        load.wait()
    for u in range(units):
        at = slice(u * LANES, (u + 1) * LANES)
        masked = blocks[c, z, y, :, at] * keep(in_ref, u)
        blocks[c, z, y, :, at] = masked
        row_parts[n, :, at] = masked

    met = 1 + 1 + len(others) + has_up.astype(jnp.int32) + has_down.astype(jnp.int32)
    pl.semaphore_wait(barrier, met)

    low, rest = pl.ds(0, cut[-1]), pl.ds(cut[-1], rows - cut[-1])

    def piece(core, plane, yy, part):
        return blocks.at[core, plane, yy, pl.ds(cut[part], cut[part + 1] - cut[part]), :]

    def both_rest(core, plane):
        return blocks.at[core, plane, :, rest, :]

    def copy(kind, ref, plane, number):
        via = {UP: 0, DOWN: 0, ACROSS: 1, SIBLING: 2}[kind]
        return pltpu.make_async_remote_copy(
            src_ref=ref,
            dst_ref=ref,
            send_sem=send_sem.at[kind, plane, number],
            recv_sem=recv_sem.at[via, plane, number],
            device_id=partner(kind),
            device_id_type=MESH,
        )

    def start(kind, ref, plane, number):
        one = copy(kind, ref, plane, number)
        if kind == UP:
            pl.when(has_up)(one.start)
        elif kind == DOWN:
            pl.when(has_down)(one.start)
        else:
            one.start()

    def finish(kind, ref, plane, number):
        one = copy(kind, ref, plane, number)
        if kind == UP:
            pl.when(has_up)(one.wait_send)
        elif kind == DOWN:
            pl.when(has_down)(one.wait_send)
        else:
            one.wait_send()

    def arrive(kind, ref, plane, number):
        copy(kind, ref, plane, number).wait_recv()

    def nothing(*_):
        pass

    def row_copy(other):
        return pltpu.make_async_remote_copy(
            src_ref=blocks.at[c, z, y],
            dst_ref=row_parts.at[n],
            send_sem=row_send.at[other],
            recv_sem=row_recv.at[n],
            device_id=(other, w),
            device_id_type=MESH,
        )

    def row_arrival(other):
        return pltpu.make_async_remote_copy(
            src_ref=blocks.at[c, z, y],
            dst_ref=row_parts.at[other],
            send_sem=row_send.at[other],
            recv_sem=row_recv.at[other],
            device_id=(other, w),
            device_id_type=MESH,
        )

    def own(act):
        act(ACROSS, blocks.at[c, z, y, rest, :], z, pieces)
        for part in range(pieces):
            ref = piece(c, z, y, part)
            for kind in (UP, DOWN, ACROSS):
                act(kind, ref, z, part)
        act(SIBLING, blocks.at[c, z, y, low, :], z, 0)

    def beside(wait, act):
        wait(ACROSS, blocks.at[c, z, 1 - y, rest, :], z, pieces)
        for kind in (UP, DOWN, SIBLING):
            act(kind, both_rest(c, z), z, pieces)

    def from_across(plane, wait, act):
        for part in range(pieces):
            wait(ACROSS, piece(c, plane, 1 - y, part), plane, part)
        act(SIBLING, blocks.at[c, plane, 1 - y, low, :], plane, 1)

    def sides(step, visit):
        pl.when(z >= step)(lambda: visit(z - step, UP))
        pl.when(z + step < line)(lambda: visit(z + step, DOWN))

    def along_line(step, wait, act):
        for part in range(pieces):

            def one_piece(plane, kind):
                ref = piece(c, plane, y, part)
                wait(LINE, ref, plane, part)
                act(kind, ref, plane, part)
                act(ACROSS, ref, plane, part)
                if part == pieces - 1:
                    act(SIBLING, blocks.at[c, plane, y, low, :], plane, 0)

            sides(step, one_piece)

    def rest_of_line(step, wait, act):
        def the_rest(plane, kind):
            ref = both_rest(c, plane)
            wait(LINE, ref, plane, pieces)
            act(kind, ref, plane, pieces)
            act(SIBLING, ref, plane, pieces)

        sides(step, the_rest)

    def half(plane, core):
        b_high, b_low = split(blocks[core, plane].reshape(2 * rows, cols))
        pair = left[plane, core]
        first_two = jnp.dot(pair, b_high, preferred_element_type=jnp.float32)
        term = first_two[:rows] + first_two[rows:]
        total[...] += term + jnp.dot(pair[:rows], b_low, preferred_element_type=jnp.float32)

    def multiply(plane):
        def one_half(h, carry):
            @pl.when(h == 1)
            def _():
                arrive(SIBLING, blocks.at[1 - c, plane, y, low, :], plane, 0)
                arrive(SIBLING, blocks.at[1 - c, plane, 1 - y, low, :], plane, 1)
                arrive(SIBLING, both_rest(1 - c, plane), plane, pieces)

            half(plane, (c + h) % 2)
            return carry

        lax.fori_loop(0, 2, one_half, 0)

    own(start)
    for other in others:
        row_copy(other).start()
    total[...] = jnp.zeros_like(total)
    beside(arrive, start)

    def prepare():
        for other in others:
            row_arrival(other).wait_recv()
        for g in range(narrow):
            both = jnp.concatenate(split(row_parts[g]), axis=0)
            for q in range(group // 4):
                for core in range(2):
                    begins = [(q * 4 + 2 * yy + core) * rows for yy in range(2)]
                    left[g * (group // 4) + q, core] = jnp.concatenate(
                        [both[:, begin : begin + rows] for begin in begins], axis=1
                    )

    def late(step):
        @pl.when(step == 0)
        def _():
            from_across(z, arrive, start)
            prepare()

        @pl.when(step > 0)
        def _():
            sides(step, lambda plane, kind: from_across(plane, arrive, start))

        def one_side(side, carry):
            plane = z + (2 * side - 1) * step
            live = (plane >= 0) & (plane < line) & ((step > 0) | (side == 0))
            pl.when(live)(lambda: multiply(plane))
            return carry

        lax.fori_loop(0, 2, one_side, 0)

    at_end = (z == 0) | (z == line - 1)

    def drain_line(step, carry):
        along_line(step, nothing, finish)
        rest_of_line(step, nothing, finish)
        return carry

    def turn(step, carry):
        @pl.when(step == line - 1)
        def _():
            own(finish)
            beside(nothing, finish)
            from_across(z, nothing, finish)
            lax.fori_loop(1, line - 2, drain_line, 0)

        along_line(step, arrive, start)
        pl.when(at_end)(lambda: late(step - 1))
        rest_of_line(step, arrive, start)
        pl.when(jnp.logical_not(at_end))(lambda: late(step - 1))
        return carry

    lax.fori_loop(1, line + 1, turn, 0)

    expanded = total[...]
    partial = None
    for u in range(units):
        at = slice(u * LANES, (u + 1) * LANES)
        inflated = expanded[:, at] * expanded[:, at] * keep(out_pat_ref, u)
        o_ref[:, at] = inflated
        partial = inflated if partial is None else partial + inflated
    wide_sums = jnp.broadcast_to(jnp.sum(partial, axis=1, keepdims=True), (rows, LANES))
    padded = jnp.concatenate([wide_sums, jnp.ones((LANES - rows, LANES), jnp.float32)], axis=0)
    sums[n] = padded.T[:8]

    def sum_copy(other, slot):
        return pltpu.make_async_remote_copy(
            src_ref=sums.at[n],
            dst_ref=sums.at[slot],
            send_sem=sum_send.at[other],
            recv_sem=sum_recv.at[slot],
            device_id=(other, w),
            device_id_type=MESH,
        )

    for other in others:
        sum_copy(other, n).start()

    def drain_across(step, carry):
        sides(step, lambda plane, kind: from_across(plane, nothing, finish))
        return carry

    lax.fori_loop(line - 2, line, drain_line, 0)
    lax.fori_loop(1, line, drain_across, 0)
    for other in others:
        row_copy(other).wait_send()
    for other in others:
        sum_copy(other, other).wait_recv()
    row_sum = sums[0]
    for g in range(1, narrow):
        row_sum = row_sum + sums[g]
    spread = jnp.broadcast_to(row_sum[:1], (LANES, LANES)).T[:rows]
    scale = (cols * narrow) / spread
    for u in range(units):
        at = slice(u * LANES, (u + 1) * LANES)
        o_ref[:, at] = o_ref[:, at] * scale
    for other in others:
        sum_copy(other, n).wait_send()


def body(narrow, wide, state, in_pattern, out_pattern):
    rows, cols = state.shape
    cut = (0, 3 * rows // 10, 6 * rows // 10, 8 * rows // 10)
    line = wide // 4
    hbm = pl.BlockSpec(memory_space=pltpu.HBM)
    vmem = pl.BlockSpec(memory_space=pltpu.VMEM)
    flops = 2 * rows * cols * cols * narrow
    return pl.pallas_call(
        functools.partial(kernel, narrow, wide, cut),
        out_shape=pltpu.VMEM((rows, cols), jnp.float32),
        in_specs=[hbm, hbm, hbm],
        out_specs=vmem,
        scratch_shapes=[
            pltpu.SMEM(in_pattern.shape, jnp.int32),
            pltpu.SMEM(out_pattern.shape, jnp.int32),
            pltpu.VMEM((2, line, 2, rows, cols), jnp.float32),
            pltpu.VMEM((narrow, rows, cols), jnp.float32),
            pltpu.VMEM((line, 2, 2 * rows, 2 * rows), jnp.bfloat16),
            pltpu.VMEM((rows, cols), jnp.float32),
            pltpu.VMEM((narrow, 8, LANES), jnp.float32),
            pltpu.SemaphoreType.DMA((3,)),
            pltpu.SemaphoreType.DMA((4, line, 4)),
            pltpu.SemaphoreType.DMA((3, line, 4)),
            pltpu.SemaphoreType.DMA((narrow,)),
            pltpu.SemaphoreType.DMA((narrow,)),
            pltpu.SemaphoreType.DMA((narrow,)),
            pltpu.SemaphoreType.DMA((narrow,)),
        ],
        compiler_params=pltpu.CompilerParams(
            collective_id=0, has_side_effects=True, vmem_limit_bytes=48 * 1024 * 1024
        ),
        cost_estimate=pl.CostEstimate(flops=flops, bytes_accessed=8 * rows * cols, transcendentals=0),
    )(*[pltpu.with_memory_space_constraint(a, pltpu.HBM) for a in (in_pattern, out_pattern, state)])


def solution(mesh):
    return jax.shard_map(
        functools.partial(body, mesh.shape["narrow"], mesh.shape["wide"]),
        mesh=mesh,
        in_specs=(P("wide", "narrow"), P(), P()),
        out_specs=P("wide", "narrow"),
        check_vma=False,
    )
```

```python
import functools

import jax
import jax.numpy as jnp
from jax import lax
from jax.experimental import pallas as pl
from jax.experimental.pallas import tpu as pltpu
from jax.sharding import PartitionSpec as P

BLK = 256
LANES = 128
MESH = pl.DeviceIdType.MESH
UP, DOWN, ACROSS, SIBLING = range(4)
LINE = UP


def split(value):
    high = value.astype(jnp.bfloat16)
    low = (value - high.astype(jnp.float32)).astype(jnp.bfloat16)
    return high, low


def kernel(
    narrow, wide, cut, in_hbm, out_hbm, x_hbm, o_ref,
    in_ref, out_pat_ref, blocks, row_parts, left, total, sums, load_sem, send_sem, recv_sem,
    row_send, row_recv, sum_send, sum_recv,
):
    rows, cols = x_hbm.shape
    blks = in_ref.shape[0]
    units = cols // LANES
    line = wide // 4
    pieces = len(cut) - 1
    group = wide // narrow
    n = lax.axis_index("narrow")
    w = lax.axis_index("wide")
    z, y, c = w // 4, (w // 2) % 2, w % 2

    def index(zz, yy, cc):
        return (zz * 2 + yy) * 2 + cc

    def partner(kind):
        return {
            UP: (n, index(z + 1, y, c)),
            DOWN: (n, index(z - 1, y, c)),
            ACROSS: (n, index(z, 1 - y, c)),
            SIBLING: (n, index(z, y, 1 - c)),
        }[kind]

    loads = [
        pltpu.make_async_copy(source, target, load_sem.at[i])
        for i, (source, target) in enumerate(
            [(x_hbm, blocks.at[c, z, y]), (in_hbm, in_ref), (out_hbm, out_pat_ref)]
        )
    ]
    for load in loads:
        load.start()

    has_up, has_down = z + 1 < line, z >= 1
    others = [lax.rem(n + d, narrow) for d in range(1, narrow)]

    barrier = pltpu.get_barrier_semaphore()

    def greet(device):
        pl.semaphore_signal(barrier, inc=1, device_id=device, device_id_type=MESH)

    greet(partner(ACROSS))
    greet(partner(SIBLING))
    for other in others:
        greet((other, w))

    @pl.when(has_up)
    def _():
        greet(partner(UP))

    @pl.when(has_down)
    def _():
        greet(partner(DOWN))

    first = (w * rows) // BLK
    second = jnp.minimum(first + 1, blks - 1)
    upper = lax.broadcasted_iota(jnp.int32, (rows, LANES), 0) < (first + 1) * BLK - w * rows

    def keep(pattern, u):
        col = (n * cols + u * LANES) // BLK
        return jnp.where(
            upper, pattern[first, col].astype(jnp.float32), pattern[second, col].astype(jnp.float32)
        )

    for load in loads:
        load.wait()
    for u in range(units):
        at = slice(u * LANES, (u + 1) * LANES)
        masked = blocks[c, z, y, :, at] * keep(in_ref, u)
        blocks[c, z, y, :, at] = masked
        row_parts[n, :, at] = masked

    met = 1 + 1 + len(others) + has_up.astype(jnp.int32) + has_down.astype(jnp.int32)
    pl.semaphore_wait(barrier, met)

    low, rest = pl.ds(0, cut[-1]), pl.ds(cut[-1], rows - cut[-1])

    def piece(core, plane, yy, part):
        return blocks.at[core, plane, yy, pl.ds(cut[part], cut[part + 1] - cut[part]), :]

    def both_rest(core, plane):
        return blocks.at[core, plane, :, rest, :]

    def copy(kind, ref, plane, number):
        via = {UP: 0, DOWN: 0, ACROSS: 1, SIBLING: 2}[kind]
        return pltpu.make_async_remote_copy(
            src_ref=ref,
            dst_ref=ref,
            send_sem=send_sem.at[kind, plane, number],
            recv_sem=recv_sem.at[via, plane, number],
            device_id=partner(kind),
            device_id_type=MESH,
        )

    def start(kind, ref, plane, number):
        one = copy(kind, ref, plane, number)
        if kind == UP:
            pl.when(has_up)(one.start)
        elif kind == DOWN:
            pl.when(has_down)(one.start)
        else:
            one.start()

    def finish(kind, ref, plane, number):
        one = copy(kind, ref, plane, number)
        if kind == UP:
            pl.when(has_up)(one.wait_send)
        elif kind == DOWN:
            pl.when(has_down)(one.wait_send)
        else:
            one.wait_send()

    def arrive(kind, ref, plane, number):
        copy(kind, ref, plane, number).wait_recv()

    def nothing(*_):
        pass

    def row_copy(other):
        return pltpu.make_async_remote_copy(
            src_ref=blocks.at[c, z, y],
            dst_ref=row_parts.at[n],
            send_sem=row_send.at[other],
            recv_sem=row_recv.at[n],
            device_id=(other, w),
            device_id_type=MESH,
        )

    def row_arrival(other):
        return pltpu.make_async_remote_copy(
            src_ref=blocks.at[c, z, y],
            dst_ref=row_parts.at[other],
            send_sem=row_send.at[other],
            recv_sem=row_recv.at[other],
            device_id=(other, w),
            device_id_type=MESH,
        )

    def own(act):
        act(ACROSS, blocks.at[c, z, y, rest, :], z, pieces)
        for part in range(pieces):
            ref = piece(c, z, y, part)
            for kind in (UP, DOWN, ACROSS):
                act(kind, ref, z, part)
        act(SIBLING, blocks.at[c, z, y, low, :], z, 0)

    def beside(wait, act):
        wait(ACROSS, blocks.at[c, z, 1 - y, rest, :], z, pieces)
        for kind in (UP, DOWN, SIBLING):
            act(kind, both_rest(c, z), z, pieces)

    def from_across(plane, wait, act):
        for part in range(pieces):
            wait(ACROSS, piece(c, plane, 1 - y, part), plane, part)
        act(SIBLING, blocks.at[c, plane, 1 - y, low, :], plane, 1)

    def sides(step, visit):
        pl.when(z >= step)(lambda: visit(z - step, UP))
        pl.when(z + step < line)(lambda: visit(z + step, DOWN))

    def along_line(step, wait, act):
        for part in range(pieces):

            def one_piece(plane, kind):
                ref = piece(c, plane, y, part)
                wait(LINE, ref, plane, part)
                act(kind, ref, plane, part)
                act(ACROSS, ref, plane, part)
                if part == pieces - 1:
                    act(SIBLING, blocks.at[c, plane, y, low, :], plane, 0)

            sides(step, one_piece)

    def rest_of_line(step, wait, act):
        def the_rest(plane, kind):
            ref = both_rest(c, plane)
            wait(LINE, ref, plane, pieces)
            act(kind, ref, plane, pieces)
            act(SIBLING, ref, plane, pieces)

        sides(step, the_rest)

    def half(plane, core):
        b_high, b_low = split(blocks[core, plane].reshape(2 * rows, cols))
        pair = left[plane, core]
        first_two = jnp.dot(pair, b_high, preferred_element_type=jnp.float32)
        term = first_two[:rows] + first_two[rows:]
        total[...] += term + jnp.dot(pair[:rows], b_low, preferred_element_type=jnp.float32)

    def multiply(plane):
        def one_half(h, carry):
            @pl.when(h == 1)
            def _():
                arrive(SIBLING, blocks.at[1 - c, plane, y, low, :], plane, 0)
                arrive(SIBLING, blocks.at[1 - c, plane, 1 - y, low, :], plane, 1)
                arrive(SIBLING, both_rest(1 - c, plane), plane, pieces)

            half(plane, (c + h) % 2)
            return carry

        lax.fori_loop(0, 2, one_half, 0)

    own(start)
    for other in others:
        row_copy(other).start()
    total[...] = jnp.zeros_like(total)
    beside(arrive, start)

    def prepare():
        for other in others:
            row_arrival(other).wait_recv()
        for g in range(narrow):
            both = jnp.concatenate(split(row_parts[g]), axis=0)
            for q in range(group // 4):
                for core in range(2):
                    begins = [(q * 4 + 2 * yy + core) * rows for yy in range(2)]
                    left[g * (group // 4) + q, core] = jnp.concatenate(
                        [both[:, begin : begin + rows] for begin in begins], axis=1
                    )

    def late(step):
        @pl.when(step == 0)
        def _():
            from_across(z, arrive, start)
            prepare()

        @pl.when(step > 0)
        def _():
            sides(step, lambda plane, kind: from_across(plane, arrive, start))

        def one_side(side, carry):
            plane = z + (2 * side - 1) * step
            live = (plane >= 0) & (plane < line) & ((step > 0) | (side == 0))
            pl.when(live)(lambda: multiply(plane))
            return carry

        lax.fori_loop(0, 2, one_side, 0)

    at_end = (z == 0) | (z == line - 1)

    def drain_line(step, carry):
        along_line(step, nothing, finish)
        rest_of_line(step, nothing, finish)
        return carry

    def turn(step, carry):
        @pl.when(step == line - 1)
        def _():
            own(finish)
            beside(nothing, finish)
            from_across(z, nothing, finish)
            lax.fori_loop(1, line - 2, drain_line, 0)

        along_line(step, arrive, start)
        pl.when(at_end)(lambda: late(step - 1))
        rest_of_line(step, arrive, start)
        pl.when(jnp.logical_not(at_end))(lambda: late(step - 1))
        return carry

    lax.fori_loop(1, line + 1, turn, 0)

    expanded = total[...]
    partial = None
    for u in range(units):
        at = slice(u * LANES, (u + 1) * LANES)
        inflated = expanded[:, at] * expanded[:, at] * keep(out_pat_ref, u)
        o_ref[:, at] = inflated
        partial = inflated if partial is None else partial + inflated
    wide_sums = jnp.broadcast_to(jnp.sum(partial, axis=1, keepdims=True), (rows, LANES))
    padded = jnp.concatenate([wide_sums, jnp.ones((LANES - rows, LANES), jnp.float32)], axis=0)
    sums[n] = padded.T[:8]

    def sum_copy(other, slot):
        return pltpu.make_async_remote_copy(
            src_ref=sums.at[n],
            dst_ref=sums.at[slot],
            send_sem=sum_send.at[other],
            recv_sem=sum_recv.at[slot],
            device_id=(other, w),
            device_id_type=MESH,
        )

    for other in others:
        sum_copy(other, n).start()

    def drain_across(step, carry):
        sides(step, lambda plane, kind: from_across(plane, nothing, finish))
        return carry

    lax.fori_loop(line - 2, line, drain_line, 0)
    lax.fori_loop(1, line, drain_across, 0)
    for other in others:
        row_copy(other).wait_send()
    for other in others:
        sum_copy(other, other).wait_recv()
    row_sum = sums[0]
    for g in range(1, narrow):
        row_sum = row_sum + sums[g]
    spread = jnp.broadcast_to(row_sum[:1], (LANES, LANES)).T[:rows]
    scale = (cols * narrow) / spread
    for u in range(units):
        at = slice(u * LANES, (u + 1) * LANES)
        o_ref[:, at] = o_ref[:, at] * scale
    for other in others:
        sum_copy(other, n).wait_send()


def body(narrow, wide, state, in_pattern, out_pattern):
    rows, cols = state.shape
    cut = (0, 4 * rows // 10, 7 * rows // 10, 9 * rows // 10)
    line = wide // 4
    hbm = pl.BlockSpec(memory_space=pltpu.HBM)
    vmem = pl.BlockSpec(memory_space=pltpu.VMEM)
    flops = 2 * rows * cols * cols * narrow
    return pl.pallas_call(
        functools.partial(kernel, narrow, wide, cut),
        out_shape=pltpu.VMEM((rows, cols), jnp.float32),
        in_specs=[hbm, hbm, hbm],
        out_specs=vmem,
        scratch_shapes=[
            pltpu.SMEM(in_pattern.shape, jnp.int32),
            pltpu.SMEM(out_pattern.shape, jnp.int32),
            pltpu.VMEM((2, line, 2, rows, cols), jnp.float32),
            pltpu.VMEM((narrow, rows, cols), jnp.float32),
            pltpu.VMEM((line, 2, 2 * rows, 2 * rows), jnp.bfloat16),
            pltpu.VMEM((rows, cols), jnp.float32),
            pltpu.VMEM((narrow, 8, LANES), jnp.float32),
            pltpu.SemaphoreType.DMA((3,)),
            pltpu.SemaphoreType.DMA((4, line, 4)),
            pltpu.SemaphoreType.DMA((3, line, 4)),
            pltpu.SemaphoreType.DMA((narrow,)),
            pltpu.SemaphoreType.DMA((narrow,)),
            pltpu.SemaphoreType.DMA((narrow,)),
            pltpu.SemaphoreType.DMA((narrow,)),
        ],
        compiler_params=pltpu.CompilerParams(
            collective_id=0, has_side_effects=True, vmem_limit_bytes=48 * 1024 * 1024
        ),
        cost_estimate=pl.CostEstimate(flops=flops, bytes_accessed=8 * rows * cols, transcendentals=0),
    )(*[pltpu.with_memory_space_constraint(a, pltpu.HBM) for a in (in_pattern, out_pattern, state)])


def solution(mesh):
    return jax.shard_map(
        functools.partial(body, mesh.shape["narrow"], mesh.shape["wide"]),
        mesh=mesh,
        in_specs=(P("wide", "narrow"), P(), P()),
        out_specs=P("wide", "narrow"),
        check_vma=False,
    )
```
